32 devices in a mesh: groups: 2 (over y), track: 4 (over z), frame: 2 (over x), chan: 2 (over core).
Axes of the slice: x: 2, y: 2, z: 4, core: 2. Of those that a mesh axis runs over, the one named last changes fastest.
Arguments:
- tokens: bfloat16 [512, 16, 384], P(('groups', 'track'), 'frame', 'chan'), parts along dimension 0, may hold values from -6 to 6
- track_query: bfloat16 [512, 128], P(('groups', 'track')), parts along dimension 0, may hold values from -6 to 6
- feature_map: bfloat16 [32, 1024, 128], P(('groups', 'frame'), 'track'), parts along dimension 0, may hold values from -6 to 6
- tile_ids: int32 [4, 256, 8, 1], P(('groups', 'frame'), 'track'), parts along dimension 0, may hold values from 0 to 3; in each aligned block of 256 rows (0 to 255, 256 to 511, ..., all dimensions but the last counted through in order) at most 128 rows name the same one
- corners: int32 [4, 256, 8], P(('groups', 'frame'), 'track'), parts along dimension 0, may hold values from 0 to 99
- mlp_in: bfloat16 [49, 384], replicated, may hold values from -0.875 to 0.875
- mlp_out: bfloat16 [384, 384], P(None, 'chan'), may hold values from -0.3125 to 0.3125
- cotangent: bfloat16 [512, 16, 384], P(('groups', 'track'), 'frame', 'chan'), parts along dimension 0, may hold values from -6 to 6
Outputs:
- updated: bfloat16 [512, 16, 384], P(('groups', 'track'), 'frame', 'chan'), parts along dimension 0
- tile_grad: float32 [32, 1024, 128], P(('groups', 'frame'), 'track', 'chan'), parts along dimension 0
The draws below stay inside these ranges and needn't reach their ends.
There are 2 independent parts, one for each index of `groups`. The reference program is written for one: setup_inputs(seed, part) draws one part's arguments, and reference() takes and returns one part's arrays. A program takes and returns all parts, laid end to end along the dimension named above; an argument that names none is the same for every part. Nothing has to cross between parts.
Inputs may be any that keep to these rules, and one draw needn't show every extreme that they name: `tile_ids`: taking the first three dimensions in order, every aligned block of 256 rows names any one tile at most 128 times, a bound that some block reaches.
All inputs are finite; a program needn't handle non-finite values.
Results may differ from the reference program's by a relative error of at most 0.014.
Values may be sent and summed in bfloat16 or wider, within the bound.
A program may use at most 64 MiB of HBM per device.

```python
import math
import jax
import jax.numpy as jnp
import numpy as np
from jax import lax

D = 384
HID = 384
C = 128
TW = 16
RAD = 3
FR_DEV = 8
TRACKS = 256
FRAMES = 16
FSH = 2
TILES = 4
PIX = 256
WIN = 49
HALF = 256
CAP = 128
N_CHAN = 2


def plant(array, own_key, smallest, largest):
    dims = array.shape
    place = [jax.random.randint(jax.random.fold_in(own_key, axis), (), 0, dims[axis]) for axis in range(len(dims))]
    array = array.at[tuple(place)].set(smallest)
    longest = dims.index(max(dims))
    place[longest] = (place[longest] + 1) % dims[longest]
    return array.at[tuple(place)].set(largest)


def level_of(stream_key, shape, cuts, smallest, largest):
    def one(dim, shards_of):
        draws = jax.random.uniform(jax.random.fold_in(jax.random.fold_in(stream_key, 6), dim), (shards_of,), jnp.float32, smallest / len(cuts), largest / len(cuts))
        return jnp.repeat(jnp.exp(draws), shape[dim] // shards_of).reshape((-1,) + (1,) * (len(shape) - dim - 1))

    loudness = one(*cuts[0])
    for cut in cuts[1:]:
        loudness = loudness * one(*cut)
    return loudness


def deal_out(rng, own, number, rows, amount, top, reach, lean):
    order = jax.random.permutation(rng, amount)
    heavy_load, common = load_shares(amount, rows * top, reach, lean, True), load_shares(amount, rows * top, reach, lean, False)
    places = jnp.arange(amount)

    def named(tallies, offset_by):
        used = int((tallies > 0).sum())
        fixed = max(1, used // 4)
        passed = fixed + (places - fixed + offset_by * (used - fixed)) % max(1, amount - fixed)
        return jnp.zeros((amount,), jnp.int32).at[order[jnp.where(places < fixed, places, passed)]].set(jnp.asarray(tallies, jnp.int32))

    tallies = jnp.where(number % 4 == 0, named(heavy_load, number // 4), named(common, number - number // 4 - 1))
    mixed = jax.random.permutation(jax.random.fold_in(own, 3), amount)
    source_of, taker = mixed[0:amount // 2 * 2:2], mixed[1:amount // 2 * 2:2]
    margin = jnp.minimum(tallies[source_of] - 1, reach - tallies[taker]) // 2
    margin = jnp.where((source_of == order[0]) | (taker == order[0]) | (tallies[taker] == 0), 0, jnp.maximum(margin, 0))
    passed = jax.random.randint(jax.random.fold_in(own, 4), (amount // 2,), 0, 1 << 20) % (margin + 1)
    tallies = tallies.at[source_of].add(-passed).at[taker].add(passed)
    members = jnp.searchsorted(jnp.cumsum(tallies), jnp.arange(rows * top), side="right").astype(jnp.int32)
    table = members.reshape(top, rows).T
    table = table[jax.random.permutation(jax.random.fold_in(own, 1), rows)]
    offset_by = jax.random.randint(jax.random.fold_in(own, 2), (rows, 1), 0, top)
    return jnp.take_along_axis(table, (jnp.arange(top)[None, :] + offset_by) % top, axis=1)


def load_shares(number_of, total, most, lean, full):
    weights = [(1 << 20) // math.isqrt(rank ** lean) + 1 for rank in range(1, number_of + 1)]
    largest = most if full else min(most, max(-(-total // number_of), total * weights[0] // sum(weights)))
    least = 1 if total - largest >= number_of - 1 else 0
    counts, rest = [largest] + [least] * (number_of - 1), total - largest - least * (number_of - 1)
    while rest > 0:
        movable = [i for i in range(1, number_of) if counts[i] < largest] or [i for i in range(1, number_of) if counts[i] < most]
        mass, budget = sum([weights[i] for i in movable]), rest
        for i in movable:
            more = min(most - counts[i], max(1, budget * weights[i] // mass), rest)
            counts[i] = counts[i] + more
            rest = rest - more
    return np.array(counts)


def normal_values(stream_key, shape, scale, limit, cuts=(), kind=jnp.bfloat16):
    drawn = scale * jax.random.normal(stream_key, shape, jnp.float32)
    if cuts:
        drawn = drawn * level_of(stream_key, shape, cuts, -0.22, 0.18)
    return jnp.clip(drawn, -limit, limit).astype(kind)


def setup_inputs(seed: int = 0, part: int = 0) -> dict:
    splits = jax.random.split(jax.random.key(seed), 9)
    part_keys = jax.random.split(jax.random.fold_in(splits[8], part), 9)
    tokens = normal_values(part_keys[0], (TRACKS, FRAMES, D), 1.0, 6.0, ((0, 4), (1, 2), (2, 2)))
    track_query = normal_values(part_keys[1], (TRACKS, C), 1.0, 6.0, ((0, 4),))
    feature_map = normal_values(part_keys[2], (FRAMES, TILES * PIX, C), 1.0, 6.0, ((0, 2), (1, 4)))
    tile_ids_keys = jax.random.split(jax.random.fold_in(part_keys[3], 1), FSH * TRACKS * FR_DEV // HALF)
    tile_ids_turns = jax.random.permutation(jax.random.fold_in(part_keys[3], 3), FSH * TRACKS * FR_DEV // HALF)
    tile_ids = jax.vmap(lambda own, number: deal_out(jax.random.fold_in(part_keys[3], 2), own, number, HALF, TILES, 1, CAP, 1))(tile_ids_keys, tile_ids_turns).reshape((FSH, TRACKS, FR_DEV, 1))
    corners = plant(jax.random.randint(part_keys[4], (FSH, TRACKS, FR_DEV), 0, (TW - 2 * RAD) ** 2), jax.random.fold_in(part_keys[4], 1), 0, ((TW - 2 * RAD) ** 2) - 1).astype(jnp.int32)
    mlp_in = normal_values(splits[5], (WIN, HID), WIN ** -0.5, 0.875)
    mlp_out = normal_values(splits[6], (HID, D), HID ** -0.5, 0.3125, ((1, 2),))
    cotangent = normal_values(part_keys[7], (TRACKS, FRAMES, D), 1.0, 6.0, ((0, 4), (1, 2), (2, 2)))
    return dict(tokens=tokens, track_query=track_query, feature_map=feature_map, tile_ids=tile_ids, corners=corners, mlp_in=mlp_in, mlp_out=mlp_out, cotangent=cotangent)


def gelu_tanh(values):
    return jax.nn.gelu(values, approximate=True)

def window_base(tile_num, corner_num):
    corner_span = TW - 2 * RAD
    return tile_num * (TW * TW) + corner_num // corner_span * TW + corner_num % corner_span

def reference(tokens, track_query, feature_map, tile_ids, corners, mlp_in, mlp_out, cotangent):
    win_side = 2 * RAD + 1
    corr_scale = 1.0 / math.sqrt(C)
    tile_table = jnp.transpose(tile_ids[..., 0], (0, 2, 1)).reshape(FRAMES, TRACKS)
    corner_table = jnp.transpose(corners, (0, 2, 1)).reshape(FRAMES, TRACKS)
    token_frames = jnp.transpose(tokens, (1, 0, 2))
    grad_frames = jnp.transpose(cotangent, (1, 0, 2))
    query_wide = track_query.astype(jnp.float32)
    win_steps = jnp.arange(win_side, dtype=jnp.int32)
    chan_width = D // N_CHAN

    def one_frame(inputs):
        frame_map, tile_row, corner_row, token_row, grad_row = inputs
        base_pixel = window_base(tile_row, corner_row)
        pieces = []
        for win_row in range(win_side):
            pix_index = base_pixel[:, None] + win_row * TW + win_steps[None, :]
            feats = frame_map[pix_index].astype(jnp.float32)
            pieces.append(jnp.einsum('nsc,nc->ns', feats, query_wide))
        corr_vals = (jnp.concatenate(pieces, axis=1) * corr_scale).astype(jnp.bfloat16)
        pre_act = jnp.dot(corr_vals, mlp_in, preferred_element_type=jnp.float32)
        hidden = gelu_tanh(pre_act).astype(jnp.bfloat16)
        updated = (token_row.astype(jnp.float32) + jnp.dot(hidden, mlp_out, preferred_element_type=jnp.float32)).astype(jnp.bfloat16)
        hid_grad = jnp.zeros((TRACKS, HID), jnp.float32)
        for chan_block in range(N_CHAN):
            lower = chan_block * chan_width
            partial_value = jnp.dot(grad_row[:, lower:lower + chan_width], mlp_out[:, lower:lower + chan_width].T, preferred_element_type=jnp.float32)
            hid_grad = hid_grad + lax.optimization_barrier(partial_value.astype(jnp.bfloat16)).astype(jnp.float32)
        gelu_out, gelu_pull = jax.vjp(gelu_tanh, pre_act)
        pre_grad = gelu_pull(hid_grad)[0].astype(jnp.bfloat16)
        corr_grad = jnp.dot(pre_grad, mlp_in.T, preferred_element_type=jnp.float32).astype(jnp.bfloat16)
        corr_grad = lax.optimization_barrier(corr_grad).astype(jnp.float32)
        grad_map = jnp.zeros((TILES * TW * TW, C), jnp.float32)
        for win_row in range(win_side):
            pix_index = base_pixel[:, None] + win_row * TW + win_steps[None, :]
            picked = corr_grad[:, win_row * win_side:(win_row + 1) * win_side]
            contribution = picked[:, :, None] * query_wide[:, None, :] * corr_scale
            grad_map = grad_map.at[pix_index].add(contribution)
        return (updated, grad_map)
    updated, tile_grad = lax.map(one_frame, (feature_map, tile_table, corner_table, token_frames, grad_frames))
    return (jnp.transpose(updated, (1, 0, 2)), tile_grad)
```

```python
import functools
import math

import jax
import jax.numpy as jnp
from jax import lax
from jax.experimental import pallas as pl
from jax.experimental.pallas import tpu as pltpu
from jax.sharding import PartitionSpec as P

TW = 16
RAD = 3
SIDE = 2 * RAD + 1
SPAN = TW - 2 * RAD
BF = jnp.bfloat16
F32 = jnp.float32
I32 = jnp.int32
MESH = pl.DeviceIdType.MESH


def each(count, body):
    if count <= 8:
        for step in range(count):
            body(step)
    else:
        def step_body(step, carry):
            body(step)
            return carry

        lax.fori_loop(0, count, step_body, 0)


def iota(shape, dim):
    return lax.broadcasted_iota(I32, shape, dim)


def onehot(cond):
    return jnp.where(cond, 1.0, 0.0).astype(BF)


def mm(a, b, ca=1, cb=0):
    return lax.dot_general(a, b, (((ca,), (cb,)), ((), ())), preferred_element_type=F32)


def pick(values, index):
    return jnp.take_along_axis(values, index, axis=1, mode="promise_in_bounds")


def gelu_parts(x):
    k0 = math.sqrt(2.0 / math.pi)
    k1 = 0.044715
    sq = x * x
    th = jnp.tanh(k0 * (x + k1 * (sq * x)))
    return sq, th


def kernel(n_track, tok_ref, qry_ref, fmap_ref, tile_ref, corner_ref, win_ref, wout_ref, cot_ref,
           upd_ref, tg_ref,
           qb_ref, loc_ref, wi_ref, sendw_ref, recvw_ref, xs_ref, gh_ref, ghs_ref, gho_ref, gs_ref, recvg_ref,
           qp_ref, tgs_ref,
           q_ssem, q_rsem, w_ssem, w_rsem, g_ssem, g_rsem, x_ssem, x_rsem, h_ssem, h_rsem, t_ssem, t_rsem):
    z = lax.axis_index("track")
    c = lax.axis_index("chan")
    me = z * 2 + c
    peers = 2 * n_track
    sib = {"chan": 1 - c}
    scale = 1.0 / math.sqrt(qry_ref.shape[1])
    group = min(n_track, 4)
    chunk_rows = group * 64
    n_chunks = n_track // group

    barrier = pltpu.get_barrier_semaphore()

    def greet(step):
        peer = lax.rem(me + step + 1, peers)
        pl.semaphore_signal(barrier, inc=1, device_id={"track": peer // 2, "chan": lax.rem(peer, 2)},
                            device_id_type=MESH)

    each(peers - 1, greet)

    corner = corner_ref[...]
    crow = (corner * 205) >> 11
    base = (crow * (TW - SPAN) + corner).astype(F32).astype(BF)
    tile = tile_ref[...].astype(F32).astype(BF)
    e1 = onehot(iota((8, 128), 0) == iota((8, 128), 1))
    e2 = onehot(iota((8, 128), 0) + 8 == iota((8, 128), 1))
    qb_ref[z, :, 0:128] = qry_ref[...]
    qb_ref[z, :, 128:256] = (mm(base, e1) + mm(tile, e2)).astype(BF)

    pl.semaphore_wait(barrier, peers - 1)

    def q_copy(step, slot):
        return pltpu.make_async_remote_copy(
            src_ref=qb_ref.at[slot], dst_ref=qb_ref.at[slot], send_sem=q_ssem.at[step], recv_sem=q_rsem.at[step],
            device_id={"track": lax.rem(z + step + 1, n_track)}, device_id_type=MESH)

    each(n_track - 1, lambda step: q_copy(step, z).start())

    wout = wout_ref[...]
    rows = 256
    oth = pl.multiple_of((1 - c) * rows, rows)
    own = pl.multiple_of(c * rows, rows)
    ghs_ref[...] = mm(cot_ref[pl.ds(oth, rows), :], wout, 1, 1).astype(BF)
    h_copy = pltpu.make_async_remote_copy(src_ref=ghs_ref, dst_ref=gh_ref, send_sem=h_ssem, recv_sem=h_rsem,
                                          device_id=sib, device_id_type=MESH)
    h_copy.start()
    gho_ref[...] = mm(cot_ref[pl.ds(own, rows), :], wout, 1, 1).astype(BF)

    wst = mm(onehot((iota((128, 49), 0) & 63) == iota((128, 49), 1)), win_ref[...]).astype(BF)

    each(n_track - 1, lambda step: q_copy(step, lax.rem(z + n_track - 1 - step, n_track)).wait_recv())

    lane = iota((chunk_rows, 128), 1)
    low = lane < 64
    wlane = lane & 63
    wrow = (wlane * 37) >> 8
    off = jnp.where(wlane < SIDE * SIDE, wrow * (TW - SIDE) + wlane, 0)
    krow = iota((128, 128), 0)

    def forward(k):
        k0 = k * group
        r0 = k * chunk_rows if isinstance(k, int) else pl.multiple_of(k * chunk_rows, chunk_rows)
        qry = qb_ref[pl.ds(k0, group), :, 0:128].reshape(chunk_rows, 128)
        tbl = qb_ref[pl.ds(k0, group), :, 128:256].reshape(chunk_rows, 128)
        for j in range(2):
            vals, locs = [], []
            for f in (j, j + 2):
                t = c * 4 + f
                sel = jnp.where(krow == t, 1.0, jnp.where(krow == t + 8, 256.0, 0.0)).astype(BF)
                loc = mm(tbl, sel).astype(I32) - z * 256
                loc_ref[f, pl.ds(r0, chunk_rows), :] = loc
                locs.append(loc)
                vals.append(mm(qry, fmap_ref[t], 1, 1) * scale)
            loc = jnp.where(low, locs[0], locs[1])
            idx = loc + off
            ix = idx & 127
            hi = (idx & 128) != 0
            got = [jnp.where(hi, pick(v[:, 128:256], ix), pick(v[:, 0:128], ix)) for v in vals]
            val = jnp.where(low, got[0], got[1])
            val = jnp.where((loc >= 0) & (loc < 256), val, 0.0).astype(BF)
            sendw_ref[pl.ds(k0, group), :, j * 32:(j + 1) * 32, :] = val.reshape(group, 2, 32, 128)

    each(n_chunks, forward)

    def w_copy(step, slot):
        peer = lax.rem(me + step + 1, peers)
        return pltpu.make_async_remote_copy(
            src_ref=sendw_ref.at[peer // 2, lax.rem(peer, 2)], dst_ref=recvw_ref.at[slot],
            send_sem=w_ssem.at[step], recv_sem=w_rsem.at[step],
            device_id={"track": peer // 2, "chan": lax.rem(peer, 2)}, device_id_type=MESH)

    each(peers - 1, lambda step: w_copy(step, me).start())
    recvw_ref[me] = sendw_ref[z, c]

    def maps(k):
        k0 = k * group
        r0 = k * chunk_rows if isinstance(k, int) else pl.multiple_of(k * chunk_rows, chunk_rows)
        qry = qb_ref[pl.ds(k0, group), :, 0:128].reshape(chunk_rows, 128)
        turn = onehot(((iota((128, 128), 0) + c * 64) & 127) == iota((128, 128), 1))
        qp_ref[pl.ds(r0, chunk_rows), :] = mm(qry, turn).astype(BF)
        for f in range(4):
            loc = loc_ref[f, pl.ds(r0, chunk_rows), :]
            for half in range(2):
                p = lane + half * 128
                dr = (p >> 4) - (loc >> 4)
                dc = (p & 15) - (loc & 15)
                ok = (dr >= 0) & (dr < SIDE) & (dc >= 0) & (dc < SIDE)
                wi_ref[f, half, pl.ds(r0, chunk_rows), :] = jnp.where(ok, dr * SIDE + dc + 64 * (f // 2), -1)

    each(n_chunks, maps)

    each(peers - 1, lambda step: w_copy(step, lax.rem(me + peers - 1 - step, peers)).wait_recv())

    def gathered(part):
        if n_track <= 8:
            total = recvw_ref[part].astype(F32)
            for src in range(1, n_track):
                total = total + recvw_ref[src * 2 + part].astype(F32)
            return total
        return lax.fori_loop(0, n_track, lambda src, acc: acc + recvw_ref[src * 2 + part].astype(F32),
                             jnp.zeros((64, 128), F32))

    for part in range(2):
        xs_ref[0, part * 64:(part + 1) * 64, :] = gathered(part).astype(BF)
    x_copy = pltpu.make_async_remote_copy(src_ref=xs_ref.at[0], dst_ref=xs_ref.at[1], send_sem=x_ssem,
                                          recv_sem=x_rsem, device_id=sib, device_id_type=MESH)
    x_copy.start()

    tok_row, tok_col = iota((256, 128), 0), iota((256, 128), 1)
    t_of = tok_row & 7
    spread = onehot(tok_col == ((t_of >> 2) << 6) + ((t_of & 1) << 5) + (tok_row >> 3))
    keep = ((t_of >> 1) & 1) == (tok_col >> 6)
    q_row, q_col = iota((128, 256), 0), iota((128, 256), 1)
    u_of = q_col & 7
    fold = onehot(q_row == ((u_of >> 2) << 6) + ((u_of & 1) << 5) + (q_col >> 3))

    def first_layer(slot):
        return mm(jnp.where(keep, mm(spread, xs_ref[slot]), 0.0).astype(BF), wst)

    def finish(pre, th, start):
        hidden = (0.5 * pre * (1.0 + th)).astype(BF)
        upd_ref[pl.ds(start, rows), :] = (tok_ref[pl.ds(start, rows), :].astype(F32) + mm(hidden, wout)).astype(BF)

    pre = first_layer(0)
    sq, th = gelu_parts(pre)
    slope = 0.5 * (1.0 + th) + (0.5 * math.sqrt(2.0 / math.pi)) * pre * (1.0 - th * th) * (1.0 + 3 * 0.044715 * sq)
    h_copy.wait_recv()
    hid = gho_ref[...].astype(F32) + gh_ref[...].astype(F32)
    pre_grad = (hid * slope).astype(BF)
    cg = jnp.where(keep, mm(pre_grad, wst, 1, 1), 0.0).astype(BF)
    gs_ref[...] = mm(fold, cg).astype(BF).reshape(2, 64, 128)

    def g_copy(step, slot):
        peer = lax.rem(me + step + 1, peers)
        return pltpu.make_async_remote_copy(
            src_ref=gs_ref.at[lax.rem(peer, 2)], dst_ref=recvg_ref.at[slot],
            send_sem=g_ssem.at[step], recv_sem=g_rsem.at[step],
            device_id={"track": peer // 2, "chan": lax.rem(peer, 2)}, device_id_type=MESH)

    each(peers - 1, lambda step: g_copy(step, me).start())
    recvg_ref[me] = gs_ref[c]

    finish(pre, th, own)
    x_copy.wait_recv()
    pre = first_layer(1)
    sq, th = gelu_parts(pre)
    finish(pre, th, oth)

    each(peers - 1, lambda step: g_copy(step, lax.rem(me + peers - 1 - step, peers)).wait_recv())

    t_copies = []
    for f in range(4):
        j = f % 2

        def cells(k, f=f, j=j):
            k0 = k * group * 2
            r0 = k * chunk_rows if isinstance(k, int) else pl.multiple_of(k * chunk_rows, chunk_rows)
            g = recvg_ref[pl.ds(k0, group * 2), j * 32:(j + 1) * 32, :].reshape(chunk_rows, 128).astype(F32)
            qp = qp_ref[pl.ds(r0, chunk_rows), :]
            halves = []
            for half in range(2):
                wi = wi_ref[f, half, pl.ds(r0, chunk_rows), :]
                placed = jnp.where(wi >= 0, pick(g, wi & 127), 0.0).astype(BF)
                halves.append(mm(placed, qp, 0, 0))
            return jnp.concatenate(halves, axis=0)

        if n_chunks == 1:
            total = cells(0)
        else:
            total = lax.fori_loop(0, n_chunks, lambda k, acc: acc + cells(k), jnp.zeros((256, 128), F32))
        total = total * scale
        t = c * 4 + f
        tg_ref[t] = total[:, 0:64]
        tgs_ref[f] = total[:, 64:128]
        copy = pltpu.make_async_remote_copy(src_ref=tgs_ref.at[f], dst_ref=tg_ref.at[t], send_sem=t_ssem.at[f],
                                            recv_sem=t_rsem.at[f], device_id=sib, device_id_type=MESH)
        copy.start()
        t_copies.append(copy)

    each(n_track - 1, lambda step: q_copy(step, z).wait_send())
    h_copy.wait_send()
    each(peers - 1, lambda step: w_copy(step, me).wait_send())
    x_copy.wait_send()
    each(peers - 1, lambda step: g_copy(step, me).wait_send())
    for f in range(4):
        t_copies[f].wait_send()
        pltpu.make_async_remote_copy(src_ref=tgs_ref.at[f], dst_ref=tg_ref.at[(1 - c) * 4 + f], send_sem=t_ssem.at[f],
                                     recv_sem=t_rsem.at[f], device_id=sib, device_id_type=MESH).wait_recv()


def on_device(tokens, track_query, feature_map, tile_ids, corners, mlp_in, mlp_out, cotangent):
    local_tracks, local_frames, width = tokens.shape
    n_track = lax.axis_size("track")
    rows = local_tracks * local_frames
    pixels, channels = feature_map.shape[1:]
    hid = mlp_in.shape[1]
    peers = 2 * n_track
    all_tracks = n_track * local_tracks
    dma = pltpu.SemaphoreType.DMA
    vmem = pltpu.VMEM
    upd, tg = pl.pallas_call(
        functools.partial(kernel, n_track),
        out_shape=(
            jax.ShapeDtypeStruct((rows, width), BF),
            jax.ShapeDtypeStruct((local_frames, pixels, channels // 2), F32),
        ),
        in_specs=[pl.BlockSpec(memory_space=vmem)] * 8,
        out_specs=(pl.BlockSpec(memory_space=vmem), pl.BlockSpec(memory_space=vmem)),
        scratch_shapes=[
            vmem((n_track, local_tracks, 256), BF),
            vmem((4, all_tracks, 128), I32),
            vmem((4, 2, all_tracks, 128), I32),
            vmem((n_track, 2, 64, 128), BF),
            vmem((peers, 64, 128), BF),
            vmem((2, 128, 128), BF),
            vmem((256, hid), BF),
            vmem((256, hid), BF),
            vmem((256, hid), BF),
            vmem((2, 64, 128), BF),
            vmem((peers, 64, 128), BF),
            vmem((all_tracks, 128), BF),
            vmem((4, pixels, channels // 2), F32),
            dma((n_track - 1,)), dma((n_track - 1,)),
            dma((peers - 1,)), dma((peers - 1,)),
            dma((peers - 1,)), dma((peers - 1,)),
            dma, dma, dma, dma,
            dma((4,)), dma((4,)),
        ],
        compiler_params=pltpu.CompilerParams(collective_id=0, has_side_effects=True,
                                             vmem_limit_bytes=48 * 1024 * 1024),
        cost_estimate=pl.CostEstimate(flops=10**9, bytes_accessed=4 * 10**6, transcendentals=2 * 10**5),
        name="corr_step",
    )(
        tokens.reshape(rows, width), track_query, feature_map, tile_ids.reshape(local_tracks, local_frames),
        corners.reshape(local_tracks, local_frames), mlp_in, mlp_out, cotangent.reshape(rows, width),
    )
    return upd.reshape(tokens.shape), tg


def solution(mesh):
    return jax.shard_map(
        on_device,
        mesh=mesh,
        in_specs=(
            P(("groups", "track"), "frame", "chan"),
            P(("groups", "track"), None),
            P(("groups", "frame"), "track", None),
            P(("groups", "frame"), "track", None, None),
            P(("groups", "frame"), "track", None),
            P(),
            P(None, "chan"),
            P(("groups", "track"), "frame", "chan"),
        ),
        out_specs=(
            P(("groups", "track"), "frame", "chan"),
            P(("groups", "frame"), "track", "chan"),
        ),
        check_vma=False,
    )
```

```python
import functools
import math

import jax
import jax.numpy as jnp
from jax import lax
from jax.experimental import pallas as pl
from jax.experimental.pallas import tpu as pltpu
from jax.sharding import PartitionSpec as P

TW = 16
RAD = 3
SIDE = 2 * RAD + 1
SPAN = TW - 2 * RAD
BF = jnp.bfloat16
F32 = jnp.float32
I32 = jnp.int32
MESH = pl.DeviceIdType.MESH


def each(count, body):
    if count <= 8:
        for step in range(count):
            body(step)
    else:
        def step_body(step, carry):
            body(step)
            return carry

        lax.fori_loop(0, count, step_body, 0)


def iota(shape, dim):
    return lax.broadcasted_iota(I32, shape, dim)


def onehot(cond):
    return jnp.where(cond, 1.0, 0.0).astype(BF)


def mm(a, b, ca=1, cb=0):
    return lax.dot_general(a, b, (((ca,), (cb,)), ((), ())), preferred_element_type=F32)


def pick(values, index):
    return jnp.take_along_axis(values, index, axis=1, mode="promise_in_bounds")


def gelu_parts(x):
    k0 = math.sqrt(2.0 / math.pi)
    k1 = 0.044715
    sq = x * x
    th = jnp.tanh(k0 * (x + k1 * (sq * x)))
    return sq, th


def kernel(n_track, tok_hbm, qry_hbm, fmap_hbm, tile_hbm, corner_hbm, win_hbm, wout_hbm, cot_hbm,
           upd_ref, tg_ref,
           tok_ref, qry_ref, fmap_ref, tile_ref, corner_ref, win_ref, wout_ref, cot_ref,
           qb_ref, corr_ref, loc_ref, wi_ref, sendw_ref, recvw_ref, xs_ref, gh_ref, ghs_ref, gho_ref, gs_ref,
           recvg_ref, gm_ref, qt_ref, tgs_ref,
           in_sem, q_ssem, q_rsem, w_ssem, w_rsem, g_ssem, g_rsem, x_ssem, x_rsem, h_ssem, h_rsem, t_ssem, t_rsem):
    loads = [pltpu.make_async_copy(src, dst, in_sem.at[i]) for i, (src, dst) in enumerate((
        (tile_hbm, tile_ref), (corner_hbm, corner_ref), (qry_hbm, qry_ref), (cot_hbm, cot_ref), (wout_hbm, wout_ref),
        (fmap_hbm, fmap_ref), (win_hbm, win_ref), (tok_hbm, tok_ref)))]
    for load in loads:
        load.start()
    z = lax.axis_index("track")
    c = lax.axis_index("chan")
    me = z * 2 + c
    peers = 2 * n_track
    sib = {"chan": 1 - c}
    scale = 1.0 / math.sqrt(qry_ref.shape[1])
    group = min(n_track, 4)
    chunk_rows = group * 64
    n_chunks = n_track // group

    barrier = pltpu.get_barrier_semaphore()

    def greet(step):
        peer = lax.rem(me + step + 1, peers)
        pl.semaphore_signal(barrier, inc=1, device_id={"track": peer // 2, "chan": lax.rem(peer, 2)},
                            device_id_type=MESH)

    each(peers - 1, greet)

    for load in loads[:3]:
        load.wait()
    corner = corner_ref[...]
    crow = (corner * 205) >> 11
    base = (crow * (TW - SPAN) + corner).astype(F32).astype(BF)
    tile = tile_ref[:, 0, :].astype(F32).astype(BF)
    wide = onehot(iota((64, 128), 0) == iota((64, 128), 1))
    qb_ref[z, 0:64, :] = qry_ref[...]
    qb_ref[z, 64:80, :] = jnp.concatenate([mm(base, wide), mm(tile, wide)], axis=0).astype(BF)

    pl.semaphore_wait(barrier, peers - 1)

    def q_copy(step, slot):
        return pltpu.make_async_remote_copy(
            src_ref=qb_ref.at[slot], dst_ref=qb_ref.at[slot], send_sem=q_ssem.at[step], recv_sem=q_rsem.at[step],
            device_id={"track": lax.rem(z + step + 1, n_track)}, device_id_type=MESH)

    each(n_track - 1, lambda step: q_copy(step, z).start())

    for load in loads[3:]:
        load.wait()
    wout = wout_ref[...]
    rows = 256
    oth = pl.multiple_of((1 - c) * rows, rows)
    own = pl.multiple_of(c * rows, rows)
    ghs_ref[...] = mm(cot_ref[pl.ds(oth, rows), :], wout).astype(BF)
    h_copy = pltpu.make_async_remote_copy(src_ref=ghs_ref, dst_ref=gh_ref, send_sem=h_ssem, recv_sem=h_rsem,
                                          device_id=sib, device_id_type=MESH)
    h_copy.start()
    gho_ref[...] = mm(cot_ref[pl.ds(own, rows), :], wout).astype(BF)

    wst = mm(onehot((iota((128, 49), 0) & 63) == iota((128, 49), 1)), win_ref[...]).astype(BF)

    each(n_track - 1, lambda step: q_copy(step, lax.rem(z + n_track - 1 - step, n_track)).wait_recv())

    lane = iota((64, 128), 1)
    low = lane < 64
    wlane = lane & 63
    wrow = (wlane * 37) >> 8
    off = jnp.where(wlane < SIDE * SIDE, wrow * (TW - SIDE) + wlane, 0)
    krow = iota((128, 128), 0)
    eye16 = onehot(iota((16, 128), 0) == iota((16, 128), 1))

    def row_of(k, size):
        return k * size if isinstance(k, int) else pl.multiple_of(k * size, size)

    def forward(k):
        k0 = k * group
        r0 = row_of(k, chunk_rows)
        qry = qb_ref[pl.ds(k0, group), 0:64, :].reshape(chunk_rows, 128)
        tbl = jnp.concatenate([mm(qb_ref[k0 + i, 64:80, :], eye16, 0, 0)[0:64] for i in range(group)], axis=0).astype(BF)
        for f in range(4):
            t = c * 4 + f
            sel = jnp.where(krow == t, 1.0, jnp.where(krow == t + 8, 256.0, 0.0)).astype(BF)
            loc_ref[f, pl.ds(r0, chunk_rows), :] = mm(tbl, sel).astype(I32) - z * 256
            corr_ref[f, pl.ds(r0, chunk_rows), :] = mm(qry, fmap_ref[t], 1, 1) * scale

    each(n_chunks, forward)

    def w_copy(step, to, slot_z, part, sems, slot_c):
        return pltpu.make_async_remote_copy(
            src_ref=sendw_ref.at[to, part], dst_ref=recvw_ref.at[slot_z * 2 + slot_c],
            send_sem=w_ssem.at[step * 2 + part], recv_sem=w_rsem.at[step * 2 + sems],
            device_id={"track": to, "chan": part}, device_id_type=MESH)

    def windows(to):
        r0 = pl.multiple_of(to * 64, 64)
        for j in range(2):
            locs = [loc_ref[f, pl.ds(r0, 64), :] for f in (j, j + 2)]
            loc = jnp.where(low, locs[0], locs[1])
            idx = loc + off
            ix = idx & 127
            hi = (idx & 128) != 0
            got = [jnp.where(hi, pick(corr_ref[f, pl.ds(r0, 64), 128:256], ix),
                             pick(corr_ref[f, pl.ds(r0, 64), 0:128], ix)) for f in (j, j + 2)]
            val = jnp.where(low, got[0], got[1])
            val = jnp.where((loc >= 0) & (loc < 256), val, 0.0).astype(BF)
            sendw_ref[to, :, j * 32:(j + 1) * 32, :] = val.reshape(2, 32, 128)

    def w_send(step):
        to = lax.rem(z + step + 1, n_track)
        windows(to)
        for part in range(2):
            w_copy(step, to, z, part, c, c).start()

    each(n_track - 1, w_send)
    windows(z)
    last = n_track - 1

    def sib_copy(buf_src, buf_dst, ssem, rsem):
        return pltpu.make_async_remote_copy(
            src_ref=buf_src, dst_ref=buf_dst, send_sem=ssem.at[last * 2 + 1 - c], recv_sem=rsem.at[last * 2 + c],
            device_id=sib, device_id_type=MESH)

    def sib_wait(buf_src, buf_dst, ssem, rsem):
        return pltpu.make_async_remote_copy(
            src_ref=buf_src, dst_ref=buf_dst, send_sem=ssem.at[last * 2 + 1 - c], recv_sem=rsem.at[last * 2 + 1 - c],
            device_id=sib, device_id_type=MESH)

    sib_copy(sendw_ref.at[z, 1 - c], recvw_ref.at[me], w_ssem, w_rsem).start()
    recvw_ref[me] = sendw_ref[z, c]

    eye = onehot(krow == iota((128, 128), 1))
    clane = iota((chunk_rows, 128), 1)

    def maps(k):
        r0 = row_of(k, chunk_rows)
        qry = qb_ref[pl.ds(k * group, group), 0:64, :].reshape(chunk_rows, 128)
        qt_ref[:, pl.ds(r0, chunk_rows)] = mm(eye, qry, 1, 1).astype(BF)
        for f in range(4):
            loc = loc_ref[f, pl.ds(r0, chunk_rows), :]
            for half in range(2):
                p = clane + half * 128
                dr = (p >> 4) - (loc >> 4)
                dc = (p & 15) - (loc & 15)
                ok = (dr >= 0) & (dr < SIDE) & (dc >= 0) & (dc < SIDE)
                wi_ref[f, half, pl.ds(r0, chunk_rows), :] = jnp.where(ok, dr * SIDE + dc + 64 * (f // 2), -1)

    each(n_chunks, maps)

    tok_row, tok_col = iota((256, 128), 0), iota((256, 128), 1)
    t_of = tok_row & 7
    spread = onehot(tok_col == ((t_of >> 2) << 6) + ((t_of & 1) << 5) + (tok_row >> 3))
    keep = ((t_of >> 1) & 1) == (tok_col >> 6)
    q_row, q_col = iota((128, 256), 0), iota((128, 256), 1)
    u_of = q_col & 7
    fold = onehot(q_row == ((u_of >> 2) << 6) + ((u_of & 1) << 5) + (q_col >> 3))

    def w_wait(step):
        src = lax.rem(z + n_track - 1 - step, n_track)
        for part in range(2):
            w_copy(step, src, src, part, part, part).wait_recv()

    sib_wait(sendw_ref.at[z, 1 - c], recvw_ref.at[z * 2 + 1 - c], w_ssem, w_rsem).wait_recv()
    each(n_track - 1, w_wait)

    def gathered(part):
        if n_track <= 8:
            total = recvw_ref[part].astype(F32)
            for src in range(1, n_track):
                total = total + recvw_ref[src * 2 + part].astype(F32)
            return total
        return lax.fori_loop(0, n_track, lambda src, acc: acc + recvw_ref[src * 2 + part].astype(F32),
                             jnp.zeros((64, 128), F32))

    for part in range(2):
        xs_ref[0, part * 64:(part + 1) * 64, :] = gathered(part).astype(BF)
    x_copy = pltpu.make_async_remote_copy(src_ref=xs_ref.at[0], dst_ref=xs_ref.at[1], send_sem=x_ssem,
                                          recv_sem=x_rsem, device_id=sib, device_id_type=MESH)
    x_copy.start()

    def first_layer(slot):
        return mm(jnp.where(keep, mm(spread, xs_ref[slot]), 0.0).astype(BF), wst)

    def finish(pre, th, start):
        hidden = (0.5 * pre * (1.0 + th)).astype(BF)
        upd_ref[pl.ds(start, rows), :] = (
            tok_ref[pl.ds(start, rows), :].astype(F32) + mm(hidden, wout, 1, 1)).astype(BF)

    pre = first_layer(0)
    sq, th = gelu_parts(pre)
    slope = 0.5 * (1.0 + th) + (0.5 * math.sqrt(2.0 / math.pi)) * pre * (1.0 - th * th) * (1.0 + 3 * 0.044715 * sq)
    h_copy.wait_recv()
    hid = gho_ref[...].astype(F32) + gh_ref[...].astype(F32)
    pre_grad = (hid * slope).astype(BF)
    cg = jnp.where(keep, mm(pre_grad, wst, 1, 1), 0.0).astype(BF)
    gs_ref[...] = mm(fold, cg).astype(BF).reshape(2, 64, 128)

    def g_copy(step, to, slot_z, part, sems, slot_c):
        return pltpu.make_async_remote_copy(
            src_ref=gs_ref.at[part], dst_ref=recvg_ref.at[slot_z * 2 + slot_c],
            send_sem=g_ssem.at[step * 2 + part], recv_sem=g_rsem.at[step * 2 + sems],
            device_id={"track": to, "chan": part}, device_id_type=MESH)

    def g_send(step):
        for part in range(2):
            g_copy(step, lax.rem(z + step + 1, n_track), z, part, c, c).start()

    each(n_track - 1, g_send)
    sib_copy(gs_ref.at[1 - c], recvg_ref.at[me], g_ssem, g_rsem).start()
    recvg_ref[me] = gs_ref[c]

    finish(pre, th, own)
    x_copy.wait_recv()
    pre = first_layer(1)
    sq, th = gelu_parts(pre)
    finish(pre, th, oth)

    def place(src):
        r0 = pl.multiple_of(src * 64, 64)
        for f in range(4):
            j = f % 2
            g = recvg_ref[pl.ds(src * 2, 2), j * 32:(j + 1) * 32, :].reshape(64, 128).astype(F32)
            for half in range(2):
                wi = wi_ref[f, half, pl.ds(r0, 64), :]
                gm_ref[f, pl.ds(r0, 64), half * 128:(half + 1) * 128] = jnp.where(
                    wi >= 0, pick(g, wi & 127), 0.0).astype(BF)

    sib_wait(gs_ref.at[1 - c], recvg_ref.at[z * 2 + 1 - c], g_ssem, g_rsem).wait_recv()
    place(z)

    def g_take(step):
        src = lax.rem(z + n_track - 1 - step, n_track)
        for part in range(2):
            g_copy(step, src, src, part, part, part).wait_recv()
        place(src)

    each(n_track - 1, g_take)

    half_ch = tg_ref.shape[1]
    theirs = pl.multiple_of((1 - c) * half_ch, half_ch)
    mine = pl.multiple_of(c * half_ch, half_ch)

    def t_copy(f, t):
        return pltpu.make_async_remote_copy(src_ref=tgs_ref.at[f, pl.ds(theirs, half_ch), :], dst_ref=tg_ref.at[t],
                                            send_sem=t_ssem.at[f], recv_sem=t_rsem.at[f], device_id=sib,
                                            device_id_type=MESH)

    for f in range(4):
        tgs_ref[f] = mm(qt_ref[...], gm_ref[f]) * scale
        t_copy(f, c * 4 + f).start()
        tg_ref[c * 4 + f] = tgs_ref[f, pl.ds(mine, half_ch), :]

    each(n_track - 1, lambda step: q_copy(step, z).wait_send())
    h_copy.wait_send()
    x_copy.wait_send()
    sib_copy(sendw_ref.at[z, 1 - c], recvw_ref.at[me], w_ssem, w_rsem).wait_send()
    sib_copy(gs_ref.at[1 - c], recvg_ref.at[me], g_ssem, g_rsem).wait_send()

    def sent(step):
        to = lax.rem(z + step + 1, n_track)
        for part in range(2):
            w_copy(step, to, z, part, c, c).wait_send()
            g_copy(step, to, z, part, c, c).wait_send()

    each(n_track - 1, sent)
    for f in range(4):
        t_copy(f, c * 4 + f).wait_send()
        t_copy(f, (1 - c) * 4 + f).wait_recv()


def hand_out(upd_ref, tg_ref, upd_out, tg_out, sem):
    copies = [pltpu.make_async_copy(tg_ref, tg_out, sem.at[0]), pltpu.make_async_copy(upd_ref, upd_out, sem.at[1])]
    for copy in copies:
        copy.start()
    for copy in copies:
        copy.wait()


def on_device(tokens, track_query, feature_map, tile_ids, corners, mlp_in, mlp_out, cotangent):
    local_tracks, local_frames, width = tokens.shape
    n_track = lax.axis_size("track")
    rows = local_tracks * local_frames
    pixels, channels = feature_map.shape[1:]
    hid = mlp_in.shape[1]
    peers = 2 * n_track
    all_tracks = n_track * local_tracks
    dma = pltpu.SemaphoreType.DMA
    vmem = pltpu.VMEM
    args = (
        tokens.reshape(rows, width), track_query, feature_map,
        jnp.transpose(tile_ids, (0, 2, 3, 1)).reshape(local_frames, 1, local_tracks),
        jnp.transpose(corners, (0, 2, 1)).reshape(local_frames, local_tracks), mlp_in, mlp_out.T,
        cotangent.reshape(rows, width),
    )
    outs = (
        jax.ShapeDtypeStruct((rows, width), BF),
        jax.ShapeDtypeStruct((local_frames, channels // 2, pixels), F32),
    )
    upd, tg = pl.pallas_call(
        functools.partial(kernel, n_track),
        out_shape=outs,
        in_specs=[pl.BlockSpec(memory_space=pltpu.HBM)] * 8,
        out_specs=(pl.BlockSpec(memory_space=vmem), pl.BlockSpec(memory_space=vmem)),
        scratch_shapes=[vmem(arg.shape, arg.dtype) for arg in args] + [
            vmem((n_track, 80, 128), BF),
            vmem((4, all_tracks, pixels), F32),
            vmem((4, all_tracks, 128), I32),
            vmem((4, 2, all_tracks, 128), I32),
            vmem((n_track, 2, 64, 128), BF),
            vmem((peers, 64, 128), BF),
            vmem((2, 128, 128), BF),
            vmem((256, hid), BF),
            vmem((256, hid), BF),
            vmem((256, hid), BF),
            vmem((2, 64, 128), BF),
            vmem((peers, 64, 128), BF),
            vmem((4, all_tracks, pixels), BF),
            vmem((channels, all_tracks), BF),
            vmem((4, channels, pixels), F32),
            dma((8,)),
            dma((n_track - 1,)), dma((n_track - 1,)),
            dma((peers,)), dma((peers,)),
            dma((peers,)), dma((peers,)),
            dma, dma, dma, dma,
            dma((4,)), dma((4,)),
        ],
        compiler_params=pltpu.CompilerParams(collective_id=0, has_side_effects=True,
                                             vmem_limit_bytes=48 * 1024 * 1024),
        cost_estimate=pl.CostEstimate(flops=10**9, bytes_accessed=4 * 10**6, transcendentals=2 * 10**5),
        name="corr_step",
    )(*[pltpu.with_memory_space_constraint(arg, pltpu.HBM) for arg in args])
    upd, tg = pl.pallas_call(
        hand_out,
        out_shape=outs,
        in_specs=[pl.BlockSpec(memory_space=vmem)] * 2,
        out_specs=(pl.BlockSpec(memory_space=pltpu.HBM), pl.BlockSpec(memory_space=pltpu.HBM)),
        scratch_shapes=[dma((2,))],
        name="hand_out",
    )(upd, tg)
    return upd.reshape(tokens.shape), jnp.transpose(tg, (0, 2, 1))


def solution(mesh):
    return jax.shard_map(
        on_device,
        mesh=mesh,
        in_specs=(
            P(("groups", "track"), "frame", "chan"),
            P(("groups", "track"), None),
            P(("groups", "frame"), "track", None),
            P(("groups", "frame"), "track", None, None),
            P(("groups", "frame"), "track", None),
            P(),
            P(None, "chan"),
            P(("groups", "track"), "frame", "chan"),
        ),
        out_specs=(
            P(("groups", "track"), "frame", "chan"),
            P(("groups", "frame"), "track", "chan"),
        ),
        check_vma=False,
    )
```

```python
import functools
import math

import jax
import jax.numpy as jnp
from jax import lax
from jax.experimental import pallas as pl
from jax.experimental.pallas import tpu as pltpu
from jax.sharding import PartitionSpec as P

TW = 16
RAD = 3
SIDE = 2 * RAD + 1
SPAN = TW - 2 * RAD
BF = jnp.bfloat16
F32 = jnp.float32
I32 = jnp.int32
MESH = pl.DeviceIdType.MESH


def each(count, body):
    if count <= 8:
        for step in range(count):
            body(step)
    else:
        def step_body(step, carry):
            body(step)
            return carry

        lax.fori_loop(0, count, step_body, 0)


def iota(shape, dim):
    return lax.broadcasted_iota(I32, shape, dim)


def onehot(cond):
    return jnp.where(cond, 1.0, 0.0).astype(BF)


def mm(a, b, ca=1, cb=0):
    return lax.dot_general(a, b, (((ca,), (cb,)), ((), ())), preferred_element_type=F32)


def pick(values, index):
    return jnp.take_along_axis(values, index, axis=1, mode="promise_in_bounds")


def gelu_parts(x):
    k0 = math.sqrt(2.0 / math.pi)
    k1 = 0.044715
    sq = x * x
    th = jnp.tanh(k0 * (x + k1 * (sq * x)))
    return sq, th


def kernel(n_track, tok_hbm, qry_hbm, fmap_hbm, tile_hbm, corner_hbm, win_hbm, wout_hbm, cot_hbm,
           upd_hbm, tg_hbm,
           tok_ref, qry_ref, fmap_ref, tile_ref, corner_ref, win_ref, wout_ref, cot_ref,
           qb_ref, corr_ref, loc_ref, wi_ref, sendw_ref, recvw_ref, xs_ref, gh_ref, ghs_ref, gho_ref, gs_ref,
           recvg_ref, gm_ref, qt_ref, tgs_ref, upd_ref,
           in_sem, out_sem, q_ssem, q_rsem, w_ssem, w_rsem, g_ssem, g_rsem, x_ssem, x_rsem, h_ssem, h_rsem, t_ssem, t_rsem):
    loads = [pltpu.make_async_copy(src, dst, in_sem.at[i]) for i, (src, dst) in enumerate((
        (tile_hbm, tile_ref), (corner_hbm, corner_ref), (qry_hbm, qry_ref), (cot_hbm, cot_ref), (wout_hbm, wout_ref),
        (fmap_hbm, fmap_ref), (win_hbm, win_ref), (tok_hbm, tok_ref)))]
    for load in loads:
        load.start()
    z = lax.axis_index("track")
    c = lax.axis_index("chan")
    me = z * 2 + c
    peers = 2 * n_track
    sib = {"chan": 1 - c}
    scale = 1.0 / math.sqrt(qry_ref.shape[1])
    group = min(n_track, 4)
    chunk_rows = group * 64
    n_chunks = n_track // group

    barrier = pltpu.get_barrier_semaphore()

    def greet(step):
        peer = lax.rem(me + step + 1, peers)
        pl.semaphore_signal(barrier, inc=1, device_id={"track": peer // 2, "chan": lax.rem(peer, 2)},
                            device_id_type=MESH)

    each(peers - 1, greet)

    for load in loads[:3]:
        load.wait()
    corner = corner_ref[...]
    crow = (corner * 205) >> 11
    base = (crow * (TW - SPAN) + corner).astype(F32).astype(BF)
    tile = tile_ref[:, 0, :].astype(F32).astype(BF)
    wide = onehot(iota((64, 128), 0) == iota((64, 128), 1))
    qb_ref[z, 0:64, :] = qry_ref[...]
    qb_ref[z, 64:80, :] = jnp.concatenate([mm(base, wide), mm(tile, wide)], axis=0).astype(BF)

    pl.semaphore_wait(barrier, peers - 1)

    def q_copy(step, slot):
        return pltpu.make_async_remote_copy(
            src_ref=qb_ref.at[slot], dst_ref=qb_ref.at[slot], send_sem=q_ssem.at[step], recv_sem=q_rsem.at[step],
            device_id={"track": lax.rem(z + step + 1, n_track)}, device_id_type=MESH)

    each(n_track - 1, lambda step: q_copy(step, z).start())

    for load in loads[3:]:
        load.wait()
    wout = wout_ref[...]
    rows = 256
    oth = pl.multiple_of((1 - c) * rows, rows)
    own = pl.multiple_of(c * rows, rows)
    ghs_ref[...] = mm(cot_ref[pl.ds(oth, rows), :], wout).astype(BF)
    h_copy = pltpu.make_async_remote_copy(src_ref=ghs_ref, dst_ref=gh_ref, send_sem=h_ssem, recv_sem=h_rsem,
                                          device_id=sib, device_id_type=MESH)
    h_copy.start()
    gho_ref[...] = mm(cot_ref[pl.ds(own, rows), :], wout).astype(BF)

    wst = mm(onehot((iota((128, 49), 0) & 63) == iota((128, 49), 1)), win_ref[...]).astype(BF)

    each(n_track - 1, lambda step: q_copy(step, lax.rem(z + n_track - 1 - step, n_track)).wait_recv())

    lane = iota((64, 128), 1)
    low = lane < 64
    wlane = lane & 63
    wrow = (wlane * 37) >> 8
    off = jnp.where(wlane < SIDE * SIDE, wrow * (TW - SIDE) + wlane, 0)
    krow = iota((128, 128), 0)
    eye16 = onehot(iota((16, 128), 0) == iota((16, 128), 1))

    def row_of(k, size):
        return k * size if isinstance(k, int) else pl.multiple_of(k * size, size)

    def forward(k):
        k0 = k * group
        r0 = row_of(k, chunk_rows)
        qry = qb_ref[pl.ds(k0, group), 0:64, :].reshape(chunk_rows, 128)
        tbl = jnp.concatenate([mm(qb_ref[k0 + i, 64:80, :], eye16, 0, 0)[0:64] for i in range(group)], axis=0).astype(BF)
        for f in range(4):
            t = c * 4 + f
            sel = jnp.where(krow == t, 1.0, jnp.where(krow == t + 8, 256.0, 0.0)).astype(BF)
            loc_ref[f, pl.ds(r0, chunk_rows), :] = mm(tbl, sel).astype(I32) - z * 256
            corr_ref[f, pl.ds(r0, chunk_rows), :] = mm(qry, fmap_ref[t], 1, 1) * scale

    each(n_chunks, forward)

    def w_copy(step, piece, to, slot_z, part, sems, slot_c):
        return pltpu.make_async_remote_copy(
            src_ref=sendw_ref.at[to, part, piece], dst_ref=recvw_ref.at[slot_z * 2 + slot_c, piece],
            send_sem=w_ssem.at[piece, step * 2 + part], recv_sem=w_rsem.at[piece, step * 2 + sems],
            device_id={"track": to, "chan": part}, device_id_type=MESH)

    def windows(to):
        r0 = pl.multiple_of(to * 64, 64)
        for j in range(2):
            locs = [loc_ref[f, pl.ds(r0, 64), :] for f in (j, j + 2)]
            loc = jnp.where(low, locs[0], locs[1])
            idx = loc + off
            ix = idx & 127
            hi = (idx & 128) != 0
            got = [jnp.where(hi, pick(corr_ref[f, pl.ds(r0, 64), 128:256], ix),
                             pick(corr_ref[f, pl.ds(r0, 64), 0:128], ix)) for f in (j, j + 2)]
            val = jnp.where(low, got[0], got[1])
            val = jnp.where((loc >= 0) & (loc < 256), val, 0.0).astype(BF)
            sendw_ref[to, :, :, j * 16:(j + 1) * 16, :] = val.reshape(2, 2, 16, 128)

    def w_send(step):
        to = lax.rem(z + step + 1, n_track)
        windows(to)
        for part in range(2):
            w_copy(step, 0, to, z, part, c, c).start()

    def w_send_rest(step):
        for part in range(2):
            w_copy(step, 1, lax.rem(z + step + 1, n_track), z, part, c, c).start()

    last = n_track - 1

    def sib_copy(buf_src, buf_dst, ssem, rsem, piece, sems):
        return pltpu.make_async_remote_copy(
            src_ref=buf_src, dst_ref=buf_dst, send_sem=ssem.at[piece, last * 2 + 1 - c],
            recv_sem=rsem.at[piece, last * 2 + sems], device_id=sib, device_id_type=MESH)

    def w_sib(piece, slot_c):
        return sib_copy(sendw_ref.at[z, 1 - c, piece], recvw_ref.at[z * 2 + slot_c, piece], w_ssem, w_rsem, piece,
                        slot_c)

    each(n_track - 1, w_send)
    windows(z)
    w_sib(0, c).start()
    each(n_track - 1, w_send_rest)
    w_sib(1, c).start()
    recvw_ref[me] = sendw_ref[z, c]

    eye = onehot(krow == iota((128, 128), 1))
    clane = iota((chunk_rows, 128), 1)

    def maps(k):
        r0 = row_of(k, chunk_rows)
        qry = qb_ref[pl.ds(k * group, group), 0:64, :].reshape(chunk_rows, 128)
        qt_ref[:, pl.ds(r0, chunk_rows)] = mm(eye, qry, 1, 1).astype(BF)
        for f in range(4):
            loc = loc_ref[f, pl.ds(r0, chunk_rows), :]
            for half in range(2):
                p = clane + half * 128
                dr = (p >> 4) - (loc >> 4)
                dc = (p & 15) - (loc & 15)
                ok = (dr >= 0) & (dr < SIDE) & (dc >= 0) & (dc < SIDE)
                wi_ref[f, half, pl.ds(r0, chunk_rows), :] = jnp.where(ok, dr * SIDE + dc + 64 * (f // 2), -1)

    each(n_chunks, maps)

    half_rows = rows // 2
    tok_row = iota((half_rows, 64), 0)
    t_of = tok_row & 7
    spread = onehot(iota((half_rows, 64), 1) == ((t_of >> 2) << 5) + ((t_of & 1) << 4) + (tok_row >> 3))
    keep = ((iota((half_rows, 128), 0) >> 1) & 1) == (iota((half_rows, 128), 1) >> 6)
    q_col = iota((64, half_rows), 1)
    u_of = q_col & 7
    fold = onehot(iota((64, half_rows), 0) == ((u_of >> 2) << 5) + ((u_of & 1) << 4) + (q_col >> 3))

    def gathered(piece, part):
        if n_track <= 8:
            total = recvw_ref[part, piece].astype(F32)
            for src in range(1, n_track):
                total = total + recvw_ref[src * 2 + part, piece].astype(F32)
            return total
        return lax.fori_loop(0, n_track, lambda src, acc: acc + recvw_ref[src * 2 + part, piece].astype(F32),
                             jnp.zeros((32, 128), F32))

    def first_layer(slot, piece):
        return mm(jnp.where(keep, mm(spread, xs_ref[slot, piece]), 0.0).astype(BF), wst)

    def finish(pre, th, start):
        start = pl.multiple_of(start, half_rows)
        hidden = (0.5 * pre * (1.0 + th)).astype(BF)
        upd_ref[pl.ds(start, half_rows), :] = (
            tok_ref[pl.ds(start, half_rows), :].astype(F32) + mm(hidden, wout, 1, 1)).astype(BF)

    def g_copy(step, piece, to, slot_z, part, sems, slot_c):
        return pltpu.make_async_remote_copy(
            src_ref=gs_ref.at[piece, part], dst_ref=recvg_ref.at[slot_z * 2 + slot_c, piece],
            send_sem=g_ssem.at[piece, step * 2 + part], recv_sem=g_rsem.at[piece, step * 2 + sems],
            device_id={"track": to, "chan": part}, device_id_type=MESH)

    def g_sib(piece, slot_c):
        return sib_copy(gs_ref.at[piece, 1 - c], recvg_ref.at[z * 2 + slot_c, piece], g_ssem, g_rsem, piece, slot_c)

    kept = []
    for piece in range(2):
        w_sib(piece, 1 - c).wait_recv()

        def w_wait(step, piece=piece):
            src = lax.rem(z + n_track - 1 - step, n_track)
            for part in range(2):
                w_copy(step, piece, src, src, part, part, part).wait_recv()

        each(n_track - 1, w_wait)
        for part in range(2):
            xs_ref[0, piece, part * 32:(part + 1) * 32, :] = gathered(piece, part).astype(BF)
        pre = first_layer(0, piece)
        sq, th = gelu_parts(pre)
        slope = 0.5 * (1.0 + th) + (0.5 * math.sqrt(2.0 / math.pi)) * pre * (1.0 - th * th) * (
            1.0 + 3 * 0.044715 * sq)
        if piece == 0:
            h_copy.wait_recv()
        here = slice(piece * half_rows, (piece + 1) * half_rows)
        hid = gho_ref[here, :].astype(F32) + gh_ref[here, :].astype(F32)
        pre_grad = (hid * slope).astype(BF)
        cg = jnp.where(keep, mm(pre_grad, wst, 1, 1), 0.0).astype(BF)
        gs_ref[piece] = mm(fold, cg).astype(BF).reshape(2, 32, 128)

        def g_send(step, piece=piece):
            for part in range(2):
                g_copy(step, piece, lax.rem(z + step + 1, n_track), z, part, c, c).start()

        each(n_track - 1, g_send)
        g_sib(piece, c).start()
        recvg_ref[me, piece] = gs_ref[piece, c]
        kept.append((pre, th))

    x_copy = pltpu.make_async_remote_copy(src_ref=xs_ref.at[0], dst_ref=xs_ref.at[1], send_sem=x_ssem,
                                          recv_sem=x_rsem, device_id=sib, device_id_type=MESH)
    x_copy.start()
    for piece in range(2):
        finish(*kept[piece], own + piece * half_rows)
    x_copy.wait_recv()
    for piece in range(2):
        pre = first_layer(1, piece)
        finish(pre, gelu_parts(pre)[1], oth + piece * half_rows)
    upd_copy = pltpu.make_async_copy(upd_ref, upd_hbm, out_sem.at[4])
    upd_copy.start()

    def place(src):
        r0 = pl.multiple_of(src * 64, 64)
        for f in range(4):
            j = f % 2
            g = recvg_ref[pl.ds(src * 2, 2), :, j * 16:(j + 1) * 16, :].reshape(64, 128).astype(F32)
            for half in range(2):
                wi = wi_ref[f, half, pl.ds(r0, 64), :]
                gm_ref[f, pl.ds(r0, 64), half * 128:(half + 1) * 128] = jnp.where(
                    wi >= 0, pick(g, wi & 127), 0.0).astype(BF)

    for piece in range(2):
        g_sib(piece, 1 - c).wait_recv()
    place(z)

    def g_take(step):
        src = lax.rem(z + n_track - 1 - step, n_track)
        for piece in range(2):
            for part in range(2):
                g_copy(step, piece, src, src, part, part, part).wait_recv()
        place(src)

    each(n_track - 1, g_take)

    half_ch = tg_hbm.shape[1]
    theirs = pl.multiple_of((1 - c) * half_ch, half_ch)
    mine = pl.multiple_of(c * half_ch, half_ch)

    def t_copy(f, t):
        return pltpu.make_async_remote_copy(src_ref=tgs_ref.at[f, pl.ds(theirs, half_ch), :], dst_ref=tg_hbm.at[t],
                                            send_sem=t_ssem.at[f], recv_sem=t_rsem.at[f], device_id=sib,
                                            device_id_type=MESH)

    def o_copy(f):
        return pltpu.make_async_copy(tgs_ref.at[f, pl.ds(mine, half_ch), :], tg_hbm.at[c * 4 + f], out_sem.at[f])

    for f in range(4):
        tgs_ref[f] = mm(qt_ref[...], gm_ref[f]) * scale
        t_copy(f, c * 4 + f).start()
        o_copy(f).start()

    each(n_track - 1, lambda step: q_copy(step, z).wait_send())
    h_copy.wait_send()
    x_copy.wait_send()
    for piece in range(2):
        w_sib(piece, c).wait_send()
        g_sib(piece, c).wait_send()

    def sent(step):
        to = lax.rem(z + step + 1, n_track)
        for piece in range(2):
            for part in range(2):
                w_copy(step, piece, to, z, part, c, c).wait_send()
                g_copy(step, piece, to, z, part, c, c).wait_send()

    each(n_track - 1, sent)
    upd_copy.wait()
    for f in range(4):
        t_copy(f, c * 4 + f).wait_send()
        t_copy(f, (1 - c) * 4 + f).wait_recv()
        o_copy(f).wait()


def on_device(tokens, track_query, feature_map, tile_ids, corners, mlp_in, mlp_out, cotangent):
    local_tracks, local_frames, width = tokens.shape
    n_track = lax.axis_size("track")
    rows = local_tracks * local_frames
    pixels, channels = feature_map.shape[1:]
    hid = mlp_in.shape[1]
    peers = 2 * n_track
    all_tracks = n_track * local_tracks
    dma = pltpu.SemaphoreType.DMA
    vmem = pltpu.VMEM
    args = (
        tokens.reshape(rows, width), track_query, feature_map,
        jnp.transpose(tile_ids, (0, 2, 3, 1)).reshape(local_frames, 1, local_tracks),
        jnp.transpose(corners, (0, 2, 1)).reshape(local_frames, local_tracks), mlp_in, mlp_out.T,
        cotangent.reshape(rows, width),
    )
    outs = (
        jax.ShapeDtypeStruct((rows, width), BF),
        jax.ShapeDtypeStruct((local_frames, channels // 2, pixels), F32),
    )
    upd, tg = pl.pallas_call(
        functools.partial(kernel, n_track),
        out_shape=outs,
        in_specs=[pl.BlockSpec(memory_space=pltpu.HBM)] * 8,
        out_specs=(pl.BlockSpec(memory_space=pltpu.HBM), pl.BlockSpec(memory_space=pltpu.HBM)),
        scratch_shapes=[vmem(arg.shape, arg.dtype) for arg in args] + [
            vmem((n_track, 80, 128), BF),
            vmem((4, all_tracks, pixels), F32),
            vmem((4, all_tracks, 128), I32),
            vmem((4, 2, all_tracks, 128), I32),
            vmem((n_track, 2, 2, 32, 128), BF),
            vmem((peers, 2, 32, 128), BF),
            vmem((2, 2, 64, 128), BF),
            vmem((256, hid), BF),
            vmem((256, hid), BF),
            vmem((256, hid), BF),
            vmem((2, 2, 32, 128), BF),
            vmem((peers, 2, 32, 128), BF),
            vmem((4, all_tracks, pixels), BF),
            vmem((channels, all_tracks), BF),
            vmem((4, channels, pixels), F32),
            vmem((rows, width), BF),
            dma((8,)), dma((5,)),
            dma((n_track - 1,)), dma((n_track - 1,)),
            dma((2, peers)), dma((2, peers)),
            dma((2, peers)), dma((2, peers)),
            dma, dma, dma, dma,
            dma((4,)), dma((4,)),
        ],
        compiler_params=pltpu.CompilerParams(collective_id=0, has_side_effects=True,
                                             vmem_limit_bytes=48 * 1024 * 1024),
        cost_estimate=pl.CostEstimate(flops=10**9, bytes_accessed=4 * 10**6, transcendentals=2 * 10**5),
        name="corr_step",
    )(*[pltpu.with_memory_space_constraint(arg, pltpu.HBM) for arg in args])
    return upd.reshape(tokens.shape), jnp.transpose(tg, (0, 2, 1))


def solution(mesh):
    return jax.shard_map(
        on_device,
        mesh=mesh,
        in_specs=(
            P(("groups", "track"), "frame", "chan"),
            P(("groups", "track"), None),
            P(("groups", "frame"), "track", None),
            P(("groups", "frame"), "track", None, None),
            P(("groups", "frame"), "track", None),
            P(),
            P(None, "chan"),
            P(("groups", "track"), "frame", "chan"),
        ),
        out_specs=(
            P(("groups", "track"), "frame", "chan"),
            P(("groups", "frame"), "track", "chan"),
        ),
        check_vma=False,
    )
```

```python
import functools
import math

import jax
import jax.numpy as jnp
from jax import lax
from jax.experimental import pallas as pl
from jax.experimental.pallas import tpu as pltpu
from jax.sharding import PartitionSpec as P

TW = 16
RAD = 3
SIDE = 2 * RAD + 1
SPAN = TW - 2 * RAD
BF = jnp.bfloat16
F32 = jnp.float32
I32 = jnp.int32
MESH = pl.DeviceIdType.MESH


def each(count, body):
    if count <= 8:
        for step in range(count):
            body(step)
    else:
        def step_body(step, carry):
            body(step)
            return carry

        lax.fori_loop(0, count, step_body, 0)


def iota(shape, dim):
    return lax.broadcasted_iota(I32, shape, dim)


def onehot(cond):
    return jnp.where(cond, 1.0, 0.0).astype(BF)


def mm(a, b, ca=1, cb=0):
    return lax.dot_general(a, b, (((ca,), (cb,)), ((), ())), preferred_element_type=F32)


def pick(values, index):
    return jnp.take_along_axis(values, index, axis=1, mode="promise_in_bounds")


def gelu_parts(x):
    k0 = math.sqrt(2.0 / math.pi)
    k1 = 0.044715
    sq = x * x
    th = jnp.tanh(k0 * (x + k1 * (sq * x)))
    return sq, th


def kernel(n_track, tok_hbm, qry_hbm, fmap_hbm, tile_hbm, corner_hbm, win_hbm, wout_hbm, cot_hbm,
           upd_hbm, tg_hbm,
           tok_ref, qry_ref, fmap_ref, tile_ref, corner_ref, win_ref, wout_ref, cot_ref,
           qb_ref, corr_ref, loc_ref, wi_ref, sendw_ref, recvw_ref, xs_ref, gh_ref, ghs_ref, gho_ref, gs_ref,
           recvg_ref, gm_ref, qt_ref, tgs_ref, upd_ref,
           in_sem, out_sem, q_ssem, q_rsem, w_ssem, w_rsem, g_ssem, g_rsem, x_ssem, x_rsem, h_ssem, h_rsem, t_ssem, t_rsem):
    loads = [pltpu.make_async_copy(src, dst, in_sem.at[i]) for i, (src, dst) in enumerate((
        (tile_hbm, tile_ref), (corner_hbm, corner_ref), (qry_hbm, qry_ref), (cot_hbm, cot_ref), (wout_hbm, wout_ref),
        (fmap_hbm, fmap_ref), (win_hbm, win_ref), (tok_hbm, tok_ref)))]
    for load in loads:
        load.start()
    z = lax.axis_index("track")
    c = lax.axis_index("chan")
    me = z * 2 + c
    peers = 2 * n_track
    sib = {"chan": 1 - c}
    scale = 1.0 / math.sqrt(qry_ref.shape[1])
    group = min(n_track, 4)
    chunk_rows = group * 64
    n_chunks = n_track // group

    barrier = pltpu.get_barrier_semaphore()

    def greet(step):
        peer = lax.rem(me + step + 1, peers)
        pl.semaphore_signal(barrier, inc=1, device_id={"track": peer // 2, "chan": lax.rem(peer, 2)},
                            device_id_type=MESH)

    each(peers - 1, greet)

    for load in loads[:3]:
        load.wait()
    corner = corner_ref[...]
    crow = (corner * 205) >> 11
    base = (crow * (TW - SPAN) + corner).astype(F32).astype(BF)
    tile = tile_ref[:, 0, :].astype(F32).astype(BF)
    wide = onehot(iota((64, 128), 0) == iota((64, 128), 1))
    qb_ref[z, 0:64, :] = qry_ref[...]
    qb_ref[z, 64:80, :] = jnp.concatenate([mm(base, wide), mm(tile, wide)], axis=0).astype(BF)

    pl.semaphore_wait(barrier, peers - 1)

    def q_copy(step, slot):
        return pltpu.make_async_remote_copy(
            src_ref=qb_ref.at[slot], dst_ref=qb_ref.at[slot], send_sem=q_ssem.at[step], recv_sem=q_rsem.at[step],
            device_id={"track": lax.rem(z + step + 1, n_track)}, device_id_type=MESH)

    each(n_track - 1, lambda step: q_copy(step, z).start())

    for load in loads[3:5]:
        load.wait()
    wout = wout_ref[...]
    rows = 256
    oth = pl.multiple_of((1 - c) * rows, rows)
    own = pl.multiple_of(c * rows, rows)
    ghs_ref[...] = mm(cot_ref[pl.ds(oth, rows), :], wout).astype(BF)
    h_copy = pltpu.make_async_remote_copy(src_ref=ghs_ref, dst_ref=gh_ref, send_sem=h_ssem, recv_sem=h_rsem,
                                          device_id=sib, device_id_type=MESH)
    h_copy.start()
    gho_ref[...] = mm(cot_ref[pl.ds(own, rows), :], wout).astype(BF)

    for load in loads[5:]:
        load.wait()

    wst = mm(onehot((iota((128, 49), 0) & 63) == iota((128, 49), 1)), win_ref[...]).astype(BF)

    each(n_track - 1, lambda step: q_copy(step, lax.rem(z + n_track - 1 - step, n_track)).wait_recv())

    lane = iota((64, 128), 1)
    low = lane < 64
    wlane = lane & 63
    wrow = (wlane * 37) >> 8
    off = jnp.where(wlane < SIDE * SIDE, wrow * (TW - SIDE) + wlane, 0)
    krow = iota((128, 128), 0)
    eye16 = onehot(iota((16, 128), 0) == iota((16, 128), 1))

    def row_of(k, size):
        return k * size if isinstance(k, int) else pl.multiple_of(k * size, size)

    def forward(k):
        k0 = k * group
        r0 = row_of(k, chunk_rows)
        qry = qb_ref[pl.ds(k0, group), 0:64, :].reshape(chunk_rows, 128)
        tbl = jnp.concatenate([mm(qb_ref[k0 + i, 64:80, :], eye16, 0, 0)[0:64] for i in range(group)], axis=0).astype(BF)
        for f in range(4):
            t = c * 4 + f
            sel = jnp.where(krow == t, 1.0, jnp.where(krow == t + 8, 256.0, 0.0)).astype(BF)
            loc_ref[f, pl.ds(r0, chunk_rows), :] = mm(tbl, sel).astype(I32) - z * 256
            corr_ref[f, pl.ds(r0, chunk_rows), :] = mm(qry, fmap_ref[t], 1, 1) * scale

    each(n_chunks, forward)

    def w_copy(step, to, slot_z, part, sems, slot_c):
        return pltpu.make_async_remote_copy(
            src_ref=sendw_ref.at[to, part], dst_ref=recvw_ref.at[slot_z * 2 + slot_c],
            send_sem=w_ssem.at[step * 2 + part], recv_sem=w_rsem.at[step * 2 + sems],
            device_id={"track": to, "chan": part}, device_id_type=MESH)

    def windows(to):
        r0 = pl.multiple_of(to * 64, 64)
        for j in range(2):
            locs = [loc_ref[f, pl.ds(r0, 64), :] for f in (j, j + 2)]
            loc = jnp.where(low, locs[0], locs[1])
            idx = loc + off
            ix = idx & 127
            hi = (idx & 128) != 0
            got = [jnp.where(hi, pick(corr_ref[f, pl.ds(r0, 64), 128:256], ix),
                             pick(corr_ref[f, pl.ds(r0, 64), 0:128], ix)) for f in (j, j + 2)]
            val = jnp.where(low, got[0], got[1])
            val = jnp.where((loc >= 0) & (loc < 256), val, 0.0).astype(BF)
            sendw_ref[to, :, j * 32:(j + 1) * 32, :] = val.reshape(2, 32, 128)

    def w_send(step):
        to = lax.rem(z + step + 1, n_track)
        windows(to)
        for part in range(2):
            w_copy(step, to, z, part, c, c).start()

    each(n_track - 1, w_send)
    windows(z)
    last = n_track - 1

    def sib_copy(buf_src, buf_dst, ssem, rsem):
        return pltpu.make_async_remote_copy(
            src_ref=buf_src, dst_ref=buf_dst, send_sem=ssem.at[last * 2 + 1 - c], recv_sem=rsem.at[last * 2 + c],
            device_id=sib, device_id_type=MESH)

    def sib_wait(buf_src, buf_dst, ssem, rsem):
        return pltpu.make_async_remote_copy(
            src_ref=buf_src, dst_ref=buf_dst, send_sem=ssem.at[last * 2 + 1 - c], recv_sem=rsem.at[last * 2 + 1 - c],
            device_id=sib, device_id_type=MESH)

    sib_copy(sendw_ref.at[z, 1 - c], recvw_ref.at[me], w_ssem, w_rsem).start()
    recvw_ref[me] = sendw_ref[z, c]

    eye = onehot(krow == iota((128, 128), 1))
    clane = iota((chunk_rows, 128), 1)

    def maps(k):
        r0 = row_of(k, chunk_rows)
        qry = qb_ref[pl.ds(k * group, group), 0:64, :].reshape(chunk_rows, 128)
        qt_ref[:, pl.ds(r0, chunk_rows)] = mm(eye, qry, 1, 1).astype(BF)
        for f in range(4):
            loc = loc_ref[f, pl.ds(r0, chunk_rows), :]
            for half in range(2):
                p = clane + half * 128
                dr = (p >> 4) - (loc >> 4)
                dc = (p & 15) - (loc & 15)
                ok = (dr >= 0) & (dr < SIDE) & (dc >= 0) & (dc < SIDE)
                wi_ref[f, half, pl.ds(r0, chunk_rows), :] = jnp.where(ok, dr * SIDE + dc + 64 * (f // 2), -1)

    each(n_chunks, maps)

    tok_row, tok_col = iota((256, 128), 0), iota((256, 128), 1)
    t_of = tok_row & 7
    spread = onehot(tok_col == ((t_of >> 2) << 6) + ((t_of & 1) << 5) + (tok_row >> 3))
    keep = ((t_of >> 1) & 1) == (tok_col >> 6)
    q_row, q_col = iota((128, 256), 0), iota((128, 256), 1)
    u_of = q_col & 7
    fold = onehot(q_row == ((u_of >> 2) << 6) + ((u_of & 1) << 5) + (q_col >> 3))

    def w_wait(step):
        src = lax.rem(z + n_track - 1 - step, n_track)
        for part in range(2):
            w_copy(step, src, src, part, part, part).wait_recv()

    sib_wait(sendw_ref.at[z, 1 - c], recvw_ref.at[z * 2 + 1 - c], w_ssem, w_rsem).wait_recv()
    each(n_track - 1, w_wait)

    def gathered(part):
        if n_track <= 8:
            total = recvw_ref[part].astype(F32)
            for src in range(1, n_track):
                total = total + recvw_ref[src * 2 + part].astype(F32)
            return total
        return lax.fori_loop(0, n_track, lambda src, acc: acc + recvw_ref[src * 2 + part].astype(F32),
                             jnp.zeros((64, 128), F32))

    for part in range(2):
        xs_ref[0, part * 64:(part + 1) * 64, :] = gathered(part).astype(BF)
    x_copy = pltpu.make_async_remote_copy(src_ref=xs_ref.at[0], dst_ref=xs_ref.at[1], send_sem=x_ssem,
                                          recv_sem=x_rsem, device_id=sib, device_id_type=MESH)
    x_copy.start()

    def first_layer(slot):
        return mm(jnp.where(keep, mm(spread, xs_ref[slot]), 0.0).astype(BF), wst)

    def finish(pre, th, start):
        hidden = (0.5 * pre * (1.0 + th)).astype(BF)
        upd_ref[pl.ds(start, rows), :] = (
            tok_ref[pl.ds(start, rows), :].astype(F32) + mm(hidden, wout, 1, 1)).astype(BF)

    pre = first_layer(0)
    sq, th = gelu_parts(pre)
    slope = 0.5 * (1.0 + th) + (0.5 * math.sqrt(2.0 / math.pi)) * pre * (1.0 - th * th) * (1.0 + 3 * 0.044715 * sq)
    h_copy.wait_recv()
    hid = gho_ref[...].astype(F32) + gh_ref[...].astype(F32)
    pre_grad = (hid * slope).astype(BF)
    cg = jnp.where(keep, mm(pre_grad, wst, 1, 1), 0.0).astype(BF)
    gs_ref[...] = mm(fold, cg).astype(BF).reshape(2, 64, 128)

    def g_copy(step, to, slot_z, part, sems, slot_c):
        return pltpu.make_async_remote_copy(
            src_ref=gs_ref.at[part], dst_ref=recvg_ref.at[slot_z * 2 + slot_c],
            send_sem=g_ssem.at[step * 2 + part], recv_sem=g_rsem.at[step * 2 + sems],
            device_id={"track": to, "chan": part}, device_id_type=MESH)

    def g_send(step):
        for part in range(2):
            g_copy(step, lax.rem(z + step + 1, n_track), z, part, c, c).start()

    each(n_track - 1, g_send)
    sib_copy(gs_ref.at[1 - c], recvg_ref.at[me], g_ssem, g_rsem).start()
    recvg_ref[me] = gs_ref[c]

    finish(pre, th, own)
    x_copy.wait_recv()
    pre = first_layer(1)
    sq, th = gelu_parts(pre)
    finish(pre, th, oth)
    upd_copy = pltpu.make_async_copy(upd_ref, upd_hbm, out_sem.at[4])
    upd_copy.start()

    def place(src):
        r0 = pl.multiple_of(src * 64, 64)
        for f in range(4):
            j = f % 2
            g = recvg_ref[pl.ds(src * 2, 2), j * 32:(j + 1) * 32, :].reshape(64, 128).astype(F32)
            for half in range(2):
                wi = wi_ref[f, half, pl.ds(r0, 64), :]
                gm_ref[f, pl.ds(r0, 64), half * 128:(half + 1) * 128] = jnp.where(
                    wi >= 0, pick(g, wi & 127), 0.0).astype(BF)

    sib_wait(gs_ref.at[1 - c], recvg_ref.at[z * 2 + 1 - c], g_ssem, g_rsem).wait_recv()
    place(z)

    def g_take(step):
        src = lax.rem(z + n_track - 1 - step, n_track)
        for part in range(2):
            g_copy(step, src, src, part, part, part).wait_recv()
        place(src)

    each(n_track - 1, g_take)

    half_ch = tg_hbm.shape[1]
    theirs = pl.multiple_of((1 - c) * half_ch, half_ch)
    mine = pl.multiple_of(c * half_ch, half_ch)

    def t_copy(f, t):
        return pltpu.make_async_remote_copy(src_ref=tgs_ref.at[f, pl.ds(theirs, half_ch), :], dst_ref=tg_hbm.at[t],
                                            send_sem=t_ssem.at[f], recv_sem=t_rsem.at[f], device_id=sib,
                                            device_id_type=MESH)

    def o_copy(f):
        return pltpu.make_async_copy(tgs_ref.at[f, pl.ds(mine, half_ch), :], tg_hbm.at[c * 4 + f], out_sem.at[f])

    for f in range(4):
        tgs_ref[f] = mm(qt_ref[...], gm_ref[f]) * scale
        t_copy(f, c * 4 + f).start()
        o_copy(f).start()

    each(n_track - 1, lambda step: q_copy(step, z).wait_send())
    h_copy.wait_send()
    x_copy.wait_send()
    sib_copy(sendw_ref.at[z, 1 - c], recvw_ref.at[me], w_ssem, w_rsem).wait_send()
    sib_copy(gs_ref.at[1 - c], recvg_ref.at[me], g_ssem, g_rsem).wait_send()

    def sent(step):
        to = lax.rem(z + step + 1, n_track)
        for part in range(2):
            w_copy(step, to, z, part, c, c).wait_send()
            g_copy(step, to, z, part, c, c).wait_send()

    each(n_track - 1, sent)
    upd_copy.wait()
    for f in range(4):
        t_copy(f, c * 4 + f).wait_send()
        t_copy(f, (1 - c) * 4 + f).wait_recv()
        o_copy(f).wait()


def on_device(tokens, track_query, feature_map, tile_ids, corners, mlp_in, mlp_out, cotangent):
    local_tracks, local_frames, width = tokens.shape
    n_track = lax.axis_size("track")
    rows = local_tracks * local_frames
    pixels, channels = feature_map.shape[1:]
    hid = mlp_in.shape[1]
    peers = 2 * n_track
    all_tracks = n_track * local_tracks
    dma = pltpu.SemaphoreType.DMA
    vmem = pltpu.VMEM
    args = (
        tokens.reshape(rows, width), track_query, feature_map,
        jnp.transpose(tile_ids, (0, 2, 3, 1)).reshape(local_frames, 1, local_tracks),
        jnp.transpose(corners, (0, 2, 1)).reshape(local_frames, local_tracks), mlp_in, mlp_out.T,
        cotangent.reshape(rows, width),
    )
    outs = (
        jax.ShapeDtypeStruct((rows, width), BF),
        jax.ShapeDtypeStruct((local_frames, channels // 2, pixels), F32),
    )
    upd, tg = pl.pallas_call(
        functools.partial(kernel, n_track),
        out_shape=outs,
        in_specs=[pl.BlockSpec(memory_space=pltpu.HBM)] * 8,
        out_specs=(pl.BlockSpec(memory_space=pltpu.HBM), pl.BlockSpec(memory_space=pltpu.HBM)),
        scratch_shapes=[vmem(arg.shape, arg.dtype) for arg in args] + [
            vmem((n_track, 80, 128), BF),
            vmem((4, all_tracks, pixels), F32),
            vmem((4, all_tracks, 128), I32),
            vmem((4, 2, all_tracks, 128), I32),
            vmem((n_track, 2, 64, 128), BF),
            vmem((peers, 64, 128), BF),
            vmem((2, 128, 128), BF),
            vmem((256, hid), BF),
            vmem((256, hid), BF),
            vmem((256, hid), BF),
            vmem((2, 64, 128), BF),
            vmem((peers, 64, 128), BF),
            vmem((4, all_tracks, pixels), BF),
            vmem((channels, all_tracks), BF),
            vmem((4, channels, pixels), F32),
            vmem((rows, width), BF),
            dma((8,)), dma((5,)),
            dma((n_track - 1,)), dma((n_track - 1,)),
            dma((peers,)), dma((peers,)),
            dma((peers,)), dma((peers,)),
            dma, dma, dma, dma,
            dma((4,)), dma((4,)),
        ],
        compiler_params=pltpu.CompilerParams(collective_id=0, has_side_effects=True,
                                             vmem_limit_bytes=48 * 1024 * 1024),
        cost_estimate=pl.CostEstimate(flops=10**9, bytes_accessed=4 * 10**6, transcendentals=2 * 10**5),
        name="corr_step",
    )(*[pltpu.with_memory_space_constraint(arg, pltpu.HBM) for arg in args])
    return upd.reshape(tokens.shape), jnp.transpose(tg, (0, 2, 1))


def solution(mesh):
    return jax.shard_map(
        on_device,
        mesh=mesh,
        in_specs=(
            P(("groups", "track"), "frame", "chan"),
            P(("groups", "track"), None),
            P(("groups", "frame"), "track", None),
            P(("groups", "frame"), "track", None, None),
            P(("groups", "frame"), "track", None),
            P(),
            P(None, "chan"),
            P(("groups", "track"), "frame", "chan"),
        ),
        out_specs=(
            P(("groups", "track"), "frame", "chan"),
            P(("groups", "frame"), "track", "chan"),
        ),
        check_vma=False,
    )
```

```python
import functools
import math

import jax
import jax.numpy as jnp
from jax import lax
from jax.experimental import pallas as pl
from jax.experimental.pallas import tpu as pltpu
from jax.sharding import PartitionSpec as P

TW = 16
RAD = 3
SIDE = 2 * RAD + 1
SPAN = TW - 2 * RAD
BF = jnp.bfloat16
F32 = jnp.float32
I32 = jnp.int32
MESH = pl.DeviceIdType.MESH


def each(count, body):
    if count <= 8:
        for step in range(count):
            body(step)
    else:
        def step_body(step, carry):
            body(step)
            return carry

        lax.fori_loop(0, count, step_body, 0)


def iota(shape, dim):
    return lax.broadcasted_iota(I32, shape, dim)


def onehot(cond):
    return jnp.where(cond, 1.0, 0.0).astype(BF)


def mm(a, b, ca=1, cb=0):
    return lax.dot_general(a, b, (((ca,), (cb,)), ((), ())), preferred_element_type=F32)


def pick(values, index):
    return jnp.take_along_axis(values, index, axis=1, mode="promise_in_bounds")


def gelu_parts(x):
    k0 = math.sqrt(2.0 / math.pi)
    k1 = 0.044715
    sq = x * x
    th = jnp.tanh(k0 * (x + k1 * (sq * x)))
    return sq, th


def kernel(n_track, tok_hbm, qry_hbm, fmap_hbm, tile_hbm, corner_hbm, win_hbm, wout_hbm, cot_hbm,
           upd_hbm, tg_hbm,
           tok_ref, qry_ref, fmap_ref, tile_ref, corner_ref, win_ref, wout_ref, cot_ref,
           qb_ref, corr_ref, loc_ref, wi_ref, sendw_ref, recvw_ref, xs_ref, gh_ref, ghs_ref, gho_ref, gs_ref,
           recvg_ref, gm_ref, qt_ref, tgs_ref, upd_ref,
           in_sem, out_sem, q_ssem, q_rsem, w_ssem, w_rsem, g_ssem, g_rsem, x_ssem, x_rsem, h_ssem, h_rsem, t_ssem, t_rsem):
    loads = [pltpu.make_async_copy(src, dst, in_sem.at[i]) for i, (src, dst) in enumerate((
        (tile_hbm, tile_ref), (corner_hbm, corner_ref), (qry_hbm, qry_ref), (cot_hbm, cot_ref), (wout_hbm, wout_ref),
        (fmap_hbm, fmap_ref), (win_hbm, win_ref), (tok_hbm, tok_ref)))]
    for load in loads:
        load.start()
    z = lax.axis_index("track")
    c = lax.axis_index("chan")
    me = z * 2 + c
    peers = 2 * n_track
    sib = {"chan": 1 - c}
    scale = 1.0 / math.sqrt(qry_ref.shape[1])
    group = min(n_track, 4)
    chunk_rows = group * 64
    n_chunks = n_track // group

    def gap(step):
        return 1 + lax.rem(jnp.int32(step + n_track // 2 - 1), jnp.int32(n_track - 1))

    def ahead(step):
        return lax.rem(z + gap(step), n_track)

    def behind(step):
        return lax.rem(z + n_track - gap(step), n_track)

    barrier = pltpu.get_barrier_semaphore()

    def greet(step):
        peer = lax.rem(me + step + 1, peers)
        pl.semaphore_signal(barrier, inc=1, device_id={"track": peer // 2, "chan": lax.rem(peer, 2)},
                            device_id_type=MESH)

    each(peers - 1, greet)

    for load in loads[:3]:
        load.wait()
    corner = corner_ref[...]
    crow = (corner * 205) >> 11
    base = (crow * (TW - SPAN) + corner).astype(F32).astype(BF)
    tile = tile_ref[:, 0, :].astype(F32).astype(BF)
    wide = onehot(iota((64, 128), 0) == iota((64, 128), 1))
    qb_ref[z, 0:64, :] = qry_ref[...]
    qb_ref[z, 64:80, :] = jnp.concatenate([mm(base, wide), mm(tile, wide)], axis=0).astype(BF)

    pl.semaphore_wait(barrier, peers - 1)

    def q_copy(step, slot):
        return pltpu.make_async_remote_copy(
            src_ref=qb_ref.at[slot], dst_ref=qb_ref.at[slot], send_sem=q_ssem.at[step], recv_sem=q_rsem.at[step],
            device_id={"track": ahead(step)}, device_id_type=MESH)

    each(n_track - 1, lambda step: q_copy(step, z).start())

    for load in loads[3:5]:
        load.wait()
    wout = wout_ref[...]
    rows = 256
    oth = pl.multiple_of((1 - c) * rows, rows)
    own = pl.multiple_of(c * rows, rows)
    ghs_ref[...] = mm(cot_ref[pl.ds(oth, rows), :], wout).astype(BF)
    h_copy = pltpu.make_async_remote_copy(src_ref=ghs_ref, dst_ref=gh_ref, send_sem=h_ssem, recv_sem=h_rsem,
                                          device_id=sib, device_id_type=MESH)
    h_copy.start()
    gho_ref[...] = mm(cot_ref[pl.ds(own, rows), :], wout).astype(BF)

    for load in loads[5:]:
        load.wait()

    wst = mm(onehot((iota((128, 49), 0) & 63) == iota((128, 49), 1)), win_ref[...]).astype(BF)

    each(n_track - 1, lambda step: q_copy(step, behind(step)).wait_recv())

    lane = iota((64, 128), 1)
    low = lane < 64
    wlane = lane & 63
    wrow = (wlane * 37) >> 8
    off = jnp.where(wlane < SIDE * SIDE, wrow * (TW - SIDE) + wlane, 0)
    krow = iota((128, 128), 0)
    eye16 = onehot(iota((16, 128), 0) == iota((16, 128), 1))

    def row_of(k, size):
        return k * size if isinstance(k, int) else pl.multiple_of(k * size, size)

    def forward(k):
        k0 = k * group
        r0 = row_of(k, chunk_rows)
        qry = qb_ref[pl.ds(k0, group), 0:64, :].reshape(chunk_rows, 128)
        tbl = jnp.concatenate([mm(qb_ref[k0 + i, 64:80, :], eye16, 0, 0)[0:64] for i in range(group)], axis=0).astype(BF)
        for f in range(4):
            t = c * 4 + f
            sel = jnp.where(krow == t, 1.0, jnp.where(krow == t + 8, 256.0, 0.0)).astype(BF)
            loc_ref[f, pl.ds(r0, chunk_rows), :] = mm(tbl, sel).astype(I32) - z * 256
            corr_ref[f, pl.ds(r0, chunk_rows), :] = mm(qry, fmap_ref[t], 1, 1) * scale

    each(n_chunks, forward)

    def w_copy(step, to, slot_z, part, sems, slot_c):
        return pltpu.make_async_remote_copy(
            src_ref=sendw_ref.at[to, part], dst_ref=recvw_ref.at[slot_z * 2 + slot_c],
            send_sem=w_ssem.at[step * 2 + part], recv_sem=w_rsem.at[step * 2 + sems],
            device_id={"track": to, "chan": part}, device_id_type=MESH)

    def windows(to):
        r0 = pl.multiple_of(to * 64, 64)
        for j in range(2):
            locs = [loc_ref[f, pl.ds(r0, 64), :] for f in (j, j + 2)]
            loc = jnp.where(low, locs[0], locs[1])
            idx = loc + off
            ix = idx & 127
            hi = (idx & 128) != 0
            got = [jnp.where(hi, pick(corr_ref[f, pl.ds(r0, 64), 128:256], ix),
                             pick(corr_ref[f, pl.ds(r0, 64), 0:128], ix)) for f in (j, j + 2)]
            val = jnp.where(low, got[0], got[1])
            val = jnp.where((loc >= 0) & (loc < 256), val, 0.0).astype(BF)
            sendw_ref[to, :, j * 32:(j + 1) * 32, :] = val.reshape(2, 32, 128)

    def w_send(step):
        to = ahead(step)
        windows(to)
        for part in range(2):
            w_copy(step, to, z, part, c, c).start()

    each(n_track - 1, w_send)
    windows(z)
    last = n_track - 1

    def sib_copy(buf_src, buf_dst, ssem, rsem):
        return pltpu.make_async_remote_copy(
            src_ref=buf_src, dst_ref=buf_dst, send_sem=ssem.at[last * 2 + 1 - c], recv_sem=rsem.at[last * 2 + c],
            device_id=sib, device_id_type=MESH)

    def sib_wait(buf_src, buf_dst, ssem, rsem):
        return pltpu.make_async_remote_copy(
            src_ref=buf_src, dst_ref=buf_dst, send_sem=ssem.at[last * 2 + 1 - c], recv_sem=rsem.at[last * 2 + 1 - c],
            device_id=sib, device_id_type=MESH)

    sib_copy(sendw_ref.at[z, 1 - c], recvw_ref.at[me], w_ssem, w_rsem).start()
    recvw_ref[me] = sendw_ref[z, c]

    eye = onehot(krow == iota((128, 128), 1))
    clane = iota((chunk_rows, 128), 1)

    def maps(k):
        r0 = row_of(k, chunk_rows)
        qry = qb_ref[pl.ds(k * group, group), 0:64, :].reshape(chunk_rows, 128)
        qt_ref[:, pl.ds(r0, chunk_rows)] = mm(eye, qry, 1, 1).astype(BF)
        for f in range(4):
            loc = loc_ref[f, pl.ds(r0, chunk_rows), :]
            for half in range(2):
                p = clane + half * 128
                dr = (p >> 4) - (loc >> 4)
                dc = (p & 15) - (loc & 15)
                ok = (dr >= 0) & (dr < SIDE) & (dc >= 0) & (dc < SIDE)
                wi_ref[f, half, pl.ds(r0, chunk_rows), :] = jnp.where(ok, dr * SIDE + dc + 64 * (f // 2), -1)

    each(n_chunks, maps)

    tok_row, tok_col = iota((256, 128), 0), iota((256, 128), 1)
    t_of = tok_row & 7
    spread = onehot(tok_col == ((t_of >> 2) << 6) + ((t_of & 1) << 5) + (tok_row >> 3))
    keep = ((t_of >> 1) & 1) == (tok_col >> 6)
    q_row, q_col = iota((128, 256), 0), iota((128, 256), 1)
    u_of = q_col & 7
    fold = onehot(q_row == ((u_of >> 2) << 6) + ((u_of & 1) << 5) + (q_col >> 3))

    def w_wait(step):
        src = behind(step)
        for part in range(2):
            w_copy(step, src, src, part, part, part).wait_recv()

    sib_wait(sendw_ref.at[z, 1 - c], recvw_ref.at[z * 2 + 1 - c], w_ssem, w_rsem).wait_recv()
    each(n_track - 1, w_wait)

    def gathered(part):
        if n_track <= 8:
            total = recvw_ref[part].astype(F32)
            for src in range(1, n_track):
                total = total + recvw_ref[src * 2 + part].astype(F32)
            return total
        return lax.fori_loop(0, n_track, lambda src, acc: acc + recvw_ref[src * 2 + part].astype(F32),
                             jnp.zeros((64, 128), F32))

    for part in range(2):
        xs_ref[0, part * 64:(part + 1) * 64, :] = gathered(part).astype(BF)
    x_copy = pltpu.make_async_remote_copy(src_ref=xs_ref.at[0], dst_ref=xs_ref.at[1], send_sem=x_ssem,
                                          recv_sem=x_rsem, device_id=sib, device_id_type=MESH)
    x_copy.start()

    def first_layer(slot):
        return mm(jnp.where(keep, mm(spread, xs_ref[slot]), 0.0).astype(BF), wst)

    def finish(pre, th, start):
        hidden = (0.5 * pre * (1.0 + th)).astype(BF)
        upd_ref[pl.ds(start, rows), :] = (
            tok_ref[pl.ds(start, rows), :].astype(F32) + mm(hidden, wout, 1, 1)).astype(BF)

    pre = first_layer(0)
    sq, th = gelu_parts(pre)
    slope = 0.5 * (1.0 + th) + (0.5 * math.sqrt(2.0 / math.pi)) * pre * (1.0 - th * th) * (1.0 + 3 * 0.044715 * sq)
    h_copy.wait_recv()
    hid = gho_ref[...].astype(F32) + gh_ref[...].astype(F32)
    pre_grad = (hid * slope).astype(BF)
    cg = jnp.where(keep, mm(pre_grad, wst, 1, 1), 0.0).astype(BF)
    gs_ref[...] = mm(fold, cg).astype(BF).reshape(2, 64, 128)

    def g_copy(step, to, slot_z, part, sems, slot_c):
        return pltpu.make_async_remote_copy(
            src_ref=gs_ref.at[part], dst_ref=recvg_ref.at[slot_z * 2 + slot_c],
            send_sem=g_ssem.at[step * 2 + part], recv_sem=g_rsem.at[step * 2 + sems],
            device_id={"track": to, "chan": part}, device_id_type=MESH)

    def g_send(step):
        for part in range(2):
            g_copy(step, ahead(step), z, part, c, c).start()

    each(n_track - 1, g_send)
    sib_copy(gs_ref.at[1 - c], recvg_ref.at[me], g_ssem, g_rsem).start()
    recvg_ref[me] = gs_ref[c]

    finish(pre, th, own)
    x_copy.wait_recv()
    pre = first_layer(1)
    sq, th = gelu_parts(pre)
    finish(pre, th, oth)
    upd_copy = pltpu.make_async_copy(upd_ref, upd_hbm, out_sem.at[4])
    upd_copy.start()

    def place(src):
        r0 = pl.multiple_of(src * 64, 64)
        for f in range(4):
            j = f % 2
            g = recvg_ref[pl.ds(src * 2, 2), j * 32:(j + 1) * 32, :].reshape(64, 128).astype(F32)
            for half in range(2):
                wi = wi_ref[f, half, pl.ds(r0, 64), :]
                gm_ref[f, pl.ds(r0, 64), half * 128:(half + 1) * 128] = jnp.where(
                    wi >= 0, pick(g, wi & 127), 0.0).astype(BF)

    sib_wait(gs_ref.at[1 - c], recvg_ref.at[z * 2 + 1 - c], g_ssem, g_rsem).wait_recv()
    place(z)

    def g_take(step):
        src = behind(step)
        for part in range(2):
            g_copy(step, src, src, part, part, part).wait_recv()
        place(src)

    each(n_track - 1, lambda step: g_take(n_track - 2 - step))

    half_ch = tg_hbm.shape[1]
    theirs = pl.multiple_of((1 - c) * half_ch, half_ch)
    mine = pl.multiple_of(c * half_ch, half_ch)

    def t_copy(f, t):
        return pltpu.make_async_remote_copy(src_ref=tgs_ref.at[f, pl.ds(theirs, half_ch), :], dst_ref=tg_hbm.at[t],
                                            send_sem=t_ssem.at[f], recv_sem=t_rsem.at[f], device_id=sib,
                                            device_id_type=MESH)

    def o_copy(f):
        return pltpu.make_async_copy(tgs_ref.at[f, pl.ds(mine, half_ch), :], tg_hbm.at[c * 4 + f], out_sem.at[f])

    for f in range(4):
        tgs_ref[f] = mm(qt_ref[...], gm_ref[f]) * scale
        t_copy(f, c * 4 + f).start()
        o_copy(f).start()

    each(n_track - 1, lambda step: q_copy(step, z).wait_send())
    h_copy.wait_send()
    x_copy.wait_send()
    sib_copy(sendw_ref.at[z, 1 - c], recvw_ref.at[me], w_ssem, w_rsem).wait_send()
    sib_copy(gs_ref.at[1 - c], recvg_ref.at[me], g_ssem, g_rsem).wait_send()

    def sent(step):
        to = ahead(step)
        for part in range(2):
            w_copy(step, to, z, part, c, c).wait_send()
            g_copy(step, to, z, part, c, c).wait_send()

    each(n_track - 1, sent)
    upd_copy.wait()
    for f in range(4):
        t_copy(f, c * 4 + f).wait_send()
        t_copy(f, (1 - c) * 4 + f).wait_recv()
        o_copy(f).wait()


def on_device(tokens, track_query, feature_map, tile_ids, corners, mlp_in, mlp_out, cotangent):
    local_tracks, local_frames, width = tokens.shape
    n_track = lax.axis_size("track")
    rows = local_tracks * local_frames
    pixels, channels = feature_map.shape[1:]
    hid = mlp_in.shape[1]
    peers = 2 * n_track
    all_tracks = n_track * local_tracks
    dma = pltpu.SemaphoreType.DMA
    vmem = pltpu.VMEM
    args = (
        tokens.reshape(rows, width), track_query, feature_map,
        jnp.transpose(tile_ids, (0, 2, 3, 1)).reshape(local_frames, 1, local_tracks),
        jnp.transpose(corners, (0, 2, 1)).reshape(local_frames, local_tracks), mlp_in, mlp_out.T,
        cotangent.reshape(rows, width),
    )
    outs = (
        jax.ShapeDtypeStruct((rows, width), BF),
        jax.ShapeDtypeStruct((local_frames, channels // 2, pixels), F32),
    )
    upd, tg = pl.pallas_call(
        functools.partial(kernel, n_track),
        out_shape=outs,
        in_specs=[pl.BlockSpec(memory_space=pltpu.HBM)] * 8,
        out_specs=(pl.BlockSpec(memory_space=pltpu.HBM), pl.BlockSpec(memory_space=pltpu.HBM)),
        scratch_shapes=[vmem(arg.shape, arg.dtype) for arg in args] + [
            vmem((n_track, 80, 128), BF),
            vmem((4, all_tracks, pixels), F32),
            vmem((4, all_tracks, 128), I32),
            vmem((4, 2, all_tracks, 128), I32),
            vmem((n_track, 2, 64, 128), BF),
            vmem((peers, 64, 128), BF),
            vmem((2, 128, 128), BF),
            vmem((256, hid), BF),
            vmem((256, hid), BF),
            vmem((256, hid), BF),
            vmem((2, 64, 128), BF),
            vmem((peers, 64, 128), BF),
            vmem((4, all_tracks, pixels), BF),
            vmem((channels, all_tracks), BF),
            vmem((4, channels, pixels), F32),
            vmem((rows, width), BF),
            dma((8,)), dma((5,)),
            dma((n_track - 1,)), dma((n_track - 1,)),
            dma((peers,)), dma((peers,)),
            dma((peers,)), dma((peers,)),
            dma, dma, dma, dma,
            dma((4,)), dma((4,)),
        ],
        compiler_params=pltpu.CompilerParams(collective_id=0, has_side_effects=True,
                                             vmem_limit_bytes=48 * 1024 * 1024),
        cost_estimate=pl.CostEstimate(flops=10**9, bytes_accessed=4 * 10**6, transcendentals=2 * 10**5),
        name="corr_step",
    )(*[pltpu.with_memory_space_constraint(arg, pltpu.HBM) for arg in args])
    return upd.reshape(tokens.shape), jnp.transpose(tg, (0, 2, 1))


def solution(mesh):
    return jax.shard_map(
        on_device,
        mesh=mesh,
        in_specs=(
            P(("groups", "track"), "frame", "chan"),
            P(("groups", "track"), None),
            P(("groups", "frame"), "track", None),
            P(("groups", "frame"), "track", None, None),
            P(("groups", "frame"), "track", None),
            P(),
            P(None, "chan"),
            P(("groups", "track"), "frame", "chan"),
        ),
        out_specs=(
            P(("groups", "track"), "frame", "chan"),
            P(("groups", "frame"), "track", "chan"),
        ),
        check_vma=False,
    )
```
